32 devices in a mesh: groups: 2 (over y), tensor: 4 (over z), dp: 2 (over x), sub: 2 (over core).
Axes of the slice: x: 2, y: 2, z: 4, core: 2. Of those that a mesh axis runs over, the one named last changes fastest.
Arguments:
- tokens: bfloat16 [4, 4, 128, 8192], P(('groups', 'dp'), None, 'tensor', 'sub'), parts along dimension 0, may hold values from -6 to 6
- cotangent: bfloat16 [4, 4, 128, 8192], P(('groups', 'dp'), None, 'tensor', 'sub'), parts along dimension 0, may hold values from -6 to 6
- w_up: bfloat16 [1024, 8192], P(('tensor', 'dp'), 'sub'), may hold values from -0.0625 to 0.0625
- w_down: bfloat16 [1024, 8192], P(('tensor', 'dp'), 'sub'), may hold values from -0.1875 to 0.1875
- active: int32 [4, 4, 1], P(('groups', 'dp')), parts along dimension 0, may hold values from 0 to 3; in each aligned block of 4 rows (0 to 3, 4 to 7, ..., all dimensions but the last counted through in order) at most 3 rows name the same one
Outputs:
- grad_tokens: bfloat16 [4, 4, 128, 8192], P(('groups', 'dp'), None, 'tensor', 'sub'), parts along dimension 0
- grad_up: bfloat16 [2048, 8192], P(('groups', 'tensor', 'dp'), 'sub'), parts along dimension 0
- grad_down: bfloat16 [2048, 8192], P(('groups', 'tensor', 'dp'), 'sub'), parts along dimension 0
The draws below stay inside these ranges and needn't reach their ends.
There are 2 independent parts, one for each index of `groups`. The reference program is written for one: setup_inputs(seed, part) draws one part's arguments, and reference() takes and returns one part's arrays. A program takes and returns all parts, laid end to end along the dimension named above; an argument that names none is the same for every part. Nothing has to cross between parts.
Inputs may be any that keep to these rules, and one draw needn't show every extreme that they name: `active`: each row lists 1 distinct blocks. Among the 4 tiles of one data replica no block is listed by more than 3 tiles, and some block is listed by exactly 3 tiles of some replica.
All inputs are finite; a program needn't handle non-finite values.
Results may differ from the reference program's by a relative error of at most 0.017.
Values may be sent and summed in bfloat16 or wider, within the bound.
No kernel may reach another device: no remote copies, remote signals or barrier semaphores. Data moves between devices by JAX's collectives and lax.ppermute only.
A program may use at most 64 MiB of HBM per device.

```python
import math
import jax
import jax.numpy as jnp
import numpy as np
from jax import lax

D = 8192
BS = 256
ROWS = 128
K = 1
MOST = 3
NB = 4
FF = 1024
TILES = 4
N_DP = 2
N_SUB = 2


def shard_levels(stream_key, extent, pieces, low, top_value):
    gain = 1.0
    for axis_at, parts in pieces:
        heights = jax.random.uniform(jax.random.fold_in(jax.random.fold_in(stream_key, 6), axis_at), (parts,), jnp.float32, low / len(pieces), top_value / len(pieces))
        gain = gain * jnp.repeat(jnp.exp(heights), extent[axis_at] // parts).reshape((-1,) + (1,) * (len(extent) - 1 - axis_at))
    return gain


def assign_block(stream_key, own, number, rows, amount, top, bound, skew):
    sequence = jax.random.permutation(stream_key, amount)
    crowded, common = portions_of(amount, rows * top, bound, skew, True), portions_of(amount, rows * top, bound, skew, False)
    places = jnp.arange(amount)

    def named(sizes, offset_by):
        used = int((sizes > 0).sum())
        fixed = max(1, used // 4)
        passed = fixed + (places - fixed + offset_by * (used - fixed)) % max(1, amount - fixed)
        return jnp.zeros((amount,), jnp.int32).at[sequence[jnp.where(places < fixed, places, passed)]].set(jnp.asarray(sizes, jnp.int32))

    sizes = jnp.where(number % 4 == 0, named(crowded, number // 4), named(common, number - number // 4 - 1))
    mixed = jax.random.permutation(jax.random.fold_in(own, 3), amount)
    source_of, taker = mixed[0:amount // 2 * 2:2], mixed[1:amount // 2 * 2:2]
    margin = jnp.minimum(sizes[source_of] - 1, bound - sizes[taker]) // 2
    margin = jnp.where((source_of == sequence[0]) | (taker == sequence[0]) | (sizes[taker] == 0), 0, jnp.maximum(margin, 0))
    passed = jax.random.randint(jax.random.fold_in(own, 4), (amount // 2,), 0, 1 << 20) % (margin + 1)
    sizes = sizes.at[source_of].add(-passed).at[taker].add(passed)
    items = jnp.searchsorted(jnp.cumsum(sizes), jnp.arange(rows * top), side="right").astype(jnp.int32)
    grid = items.reshape(top, rows).T
    grid = grid[jax.random.permutation(jax.random.fold_in(own, 1), rows)]
    offset_by = jax.random.randint(jax.random.fold_in(own, 2), (rows, 1), 0, top)
    return jnp.take_along_axis(grid, (jnp.arange(top)[None, :] + offset_by) % top, axis=1)


def portions_of(amount, total, most, skew, full):
    loads = [(1 << 20) // math.isqrt(standing ** skew) + 1 for standing in range(1, amount + 1)]
    largest = most if full else min(most, max(-(-total // amount), total * loads[0] // sum(loads)))
    least = 1 if total - largest >= amount - 1 else 0
    given, spare = [largest] + [least] * (amount - 1), total - largest - least * (amount - 1)
    while spare > 0:
        candidates = [i for i in range(1, amount) if given[i] < largest] or [i for i in range(1, amount) if given[i] < most]
        pool, budget = sum([loads[i] for i in candidates]), spare
        for i in candidates:
            addition = min(most - given[i], max(1, budget * loads[i] // pool), spare)
            given[i] = given[i] + addition
            spare = spare - addition
    return np.array(given)


def normal_values(key, dims, scale, reach, cuts=(), kind=jnp.bfloat16):
    gain = shard_levels(key, dims, cuts, -0.22, 0.18) if cuts else 1.0
    array = jax.random.normal(key, dims, jnp.float32) * scale * gain
    return jnp.minimum(jnp.maximum(array, -reach), reach).astype(kind)


def setup_inputs(seed: int = 0, part: int = 0) -> dict:
    splits = jax.random.split(jax.random.key(seed), 6)
    part_splits = jax.random.split(jax.random.fold_in(splits[5], part), 6)
    tokens = normal_values(part_splits[0], (N_DP, TILES, ROWS, D), 1.0, 6.0, ((0, 2), (2, 4), (3, 2)))
    cotangent = normal_values(part_splits[1], (N_DP, TILES, ROWS, D), 1.0, 6.0, ((0, 2), (2, 4), (3, 2)))
    w_up = normal_values(splits[2], (FF, D), D ** -0.5, 0.0625, ((0, 8), (1, 2)))
    w_down = normal_values(splits[3], (FF, D), FF ** -0.5, 0.1875, ((0, 8), (1, 2)))
    active_keys = jax.random.split(jax.random.fold_in(part_splits[4], 1), N_DP * TILES // TILES)
    active_turns = jax.random.permutation(jax.random.fold_in(part_splits[4], 3), N_DP * TILES // TILES)
    active = jax.vmap(lambda own, number: assign_block(jax.random.fold_in(part_splits[4], 2), own, number, TILES, NB, K, MOST, 2))(active_keys, active_turns).reshape((N_DP, TILES, K))
    return {"tokens": tokens, "cotangent": cotangent, "w_up": w_up, "w_down": w_down, "active": active}


def reference(tokens, cotangent, w_up, w_down, active):
    halves = N_SUB
    half_width = D // N_SUB
    up_blocks = w_up.reshape(NB, BS, D)
    down_blocks = w_down.reshape(NB, BS, D)

    def per_tile(carry, inputs):
        acc_up, acc_down = carry
        tok_now, cot_now, block_ids = inputs
        up_sel = up_blocks[block_ids].astype(jnp.float32)
        down_sel = down_blocks[block_ids].astype(jnp.float32)
        tok_f = tok_now.astype(jnp.float32)
        cot_f = cot_now.astype(jnp.float32)
        part_hidden = jnp.einsum('rhd,kfhd->hkrf', tok_f.reshape(ROWS, halves, half_width),
                                 up_sel.reshape(K, BS, halves, half_width))
        part_hidden = lax.optimization_barrier(part_hidden.astype(jnp.bfloat16)).astype(jnp.float32)
        hidden = jnp.sum(part_hidden, axis=0)
        part_grad = jnp.einsum('rhd,kfhd->hkrf', cot_f.reshape(ROWS, halves, half_width),
                               down_sel.reshape(K, BS, halves, half_width))
        part_grad = lax.optimization_barrier(part_grad.astype(jnp.bfloat16)).astype(jnp.float32)
        grad_act = jnp.sum(part_grad, axis=0)
        positive = jnp.maximum(hidden, 0.0)
        squared_activation = (positive * positive).astype(jnp.bfloat16)
        hidden_gradient = (2.0 * positive * grad_act).astype(jnp.bfloat16)
        back_rows = jnp.einsum('krf,kfd->krd', hidden_gradient.astype(jnp.float32), up_sel)
        back_rows = lax.optimization_barrier(back_rows.astype(jnp.bfloat16)).astype(jnp.float32)
        grad_tile = jnp.sum(back_rows, axis=0).astype(jnp.bfloat16)
        acc_down = acc_down.at[block_ids].add(jnp.einsum('krf,rd->kfd', squared_activation.astype(jnp.float32), cot_f))
        acc_up = acc_up.at[block_ids].add(jnp.einsum('krf,rd->kfd', hidden_gradient.astype(jnp.float32), tok_f))
        return (acc_up, acc_down), grad_tile

    def per_replica(totals, inputs):
        tok_row, cot_row, ids_row = inputs
        start = jnp.zeros((NB, BS, D), jnp.float32)
        (acc_up, acc_down), grad_tiles = lax.scan(per_tile, (start, start), (tok_row, cot_row, ids_row))
        acc_up = lax.optimization_barrier(acc_up.astype(jnp.bfloat16)).astype(jnp.float32)
        acc_down = lax.optimization_barrier(acc_down.astype(jnp.bfloat16)).astype(jnp.float32)
        return (totals[0] + acc_up, totals[1] + acc_down), grad_tiles

    empty = jnp.zeros((NB, BS, D), jnp.float32)
    (total_up, total_down), grad_tokens = lax.scan(per_replica, (empty, empty), (tokens, cotangent, active))
    grad_up = total_up.reshape(FF, D).astype(jnp.bfloat16)
    grad_down = total_down.reshape(FF, D).astype(jnp.bfloat16)
    return (grad_tokens, grad_up, grad_down)
```

```python
import functools

import jax
import jax.numpy as jnp
from jax import lax
from jax.experimental import pallas as pl
from jax.experimental.pallas import tpu as pltpu
from jax.sharding import PartitionSpec as P

MOST = 3
F32 = jnp.float32
BF16 = jnp.bfloat16


def plain(tokens, cotangent, w_up, w_down, active):
    tile_count = tokens.shape[1]
    part_rows = tokens.shape[2]
    half_width = tokens.shape[3]
    owners = lax.axis_size("tensor")
    block_ids = active[0]
    owner_list = jnp.arange(owners, dtype=jnp.int32)
    listed = jnp.any(block_ids[:, :, None] == owner_list[None, None, :], axis=1).astype(jnp.int32)
    ranking = jnp.cumsum(listed, axis=0) - 1
    slot_ids = jnp.arange(MOST, dtype=jnp.int32)
    choose = (listed.T[:, None, :] == 1) & (ranking.T[:, None, :] == slot_ids[None, :, None])
    choose_half = choose.astype(BF16)
    choose_full = choose.astype(F32)
    send_tok = jnp.einsum("omt,trd->omrd", choose_half, tokens[0], preferred_element_type=F32).astype(BF16)
    send_cot = jnp.einsum("omt,trd->omrd", choose_half, cotangent[0], preferred_element_type=F32).astype(BF16)
    up_weight_block = lax.all_gather(w_up, "dp", axis=0, tiled=True)
    down_weight_block = lax.all_gather(w_down, "dp", axis=0, tiled=True)
    slot_token = lax.all_to_all(send_tok, "tensor", split_axis=0, concat_axis=2, tiled=True)[0]
    slot_cotangent = lax.all_to_all(send_cot, "tensor", split_axis=0, concat_axis=2, tiled=True)[0]
    partial_hidden = jnp.einsum("bkn,vn->bkv", slot_token, up_weight_block, preferred_element_type=F32)
    partial_grad = jnp.einsum("bkn,vn->bkv", slot_cotangent, down_weight_block, preferred_element_type=F32)
    hidden = lax.psum(partial_hidden.astype(BF16), "sub").astype(F32)
    grad_act = lax.psum(partial_grad.astype(BF16), "sub").astype(F32)
    positive = jnp.maximum(hidden, 0.0)
    squared_activation = (positive * positive).astype(BF16)
    hidden_gradient = (2.0 * positive * grad_act).astype(BF16)
    back_rows = jnp.einsum("opl,la->opa", hidden_gradient, up_weight_block, preferred_element_type=F32).astype(BF16)
    back_rows = back_rows.reshape(MOST, owners, part_rows, half_width)
    received = lax.all_to_all(back_rows, "tensor", split_axis=1, concat_axis=1, tiled=True)
    summed = jnp.einsum("omt,mord->trd", choose_full, received.astype(F32), precision=lax.Precision.HIGHEST)
    grad_tokens = summed.astype(BF16).reshape(1, tile_count, part_rows, half_width)
    up_weight_term = jnp.einsum("epn,epk->nk", hidden_gradient, slot_token, preferred_element_type=F32)
    down_weight_term = jnp.einsum("epn,epk->nk", squared_activation, slot_cotangent, preferred_element_type=F32)
    weight_grads = lax.psum_scatter(
        jnp.concatenate([up_weight_term, down_weight_term], axis=1).astype(BF16),
        "dp",
        scatter_dimension=0,
        tiled=True,
    )
    return grad_tokens, weight_grads[:, :half_width], weight_grads[:, half_width:]


def swap(x, axis):
    return lax.ppermute(x, axis, [(0, 1), (1, 0)])


def halves(x, side):
    width = x.shape[-1] // 2
    keep = lax.dynamic_slice_in_dim(x, side * width, width, x.ndim - 1)
    pass_on = lax.dynamic_slice_in_dim(x, (1 - side) * width, width, x.ndim - 1)
    return keep, pass_on


def ordered(mine, other, side, axis):
    return jnp.where(
        side == 0,
        jnp.concatenate([mine, other], axis),
        jnp.concatenate([other, mine], axis),
    )


def dispatch_kernel(owners, slots, tiles, meta, keep, got, *outs):
    side, place = meta[0], meta[1]
    for k in range(owners):
        owner = lax.rem(place + k, owners)
        for s in range(slots):
            tile = meta[2 + owner * slots + s]
            own = lax.div(tile, tiles) == side
            at = lax.rem(tile, tiles)

            @pl.when(own)
            def _():
                outs[k][s] = keep[at]

            @pl.when(jnp.logical_not(own))
            def _():
                outs[k][s] = got[at]


def dispatch(meta, keep, got, owners, slots):
    tiles, rows, width = keep.shape
    return pl.pallas_call(
        functools.partial(dispatch_kernel, owners, slots, tiles),
        out_shape=[jax.ShapeDtypeStruct((slots, rows, width), keep.dtype)] * owners,
        in_specs=[
            pl.BlockSpec(memory_space=pltpu.SMEM),
            pl.BlockSpec(memory_space=pltpu.VMEM),
            pl.BlockSpec(memory_space=pltpu.VMEM),
        ],
        out_specs=[pl.BlockSpec(memory_space=pltpu.VMEM)] * owners,
        compiler_params=pltpu.CompilerParams(vmem_limit_bytes=32 << 20),
        cost_estimate=pl.CostEstimate(
            flops=0, bytes_accessed=4 * owners * slots * rows * width, transcendentals=0
        ),
    )(meta, keep, got)


def collect_kernel(owners, slots, tiles, meta, *rest):
    pieces, mine, other = rest[:owners], rest[owners], rest[owners + 1]
    side, place = meta[0], meta[1]
    base = 2 + owners * slots
    for r in range(2):
        out = mine if r == 0 else other
        replica = side if r == 0 else 1 - side
        for t in range(tiles):
            tile = replica * tiles + t
            k = lax.rem(meta[base + tile] - place + owners, owners)
            slot = meta[base + 2 * tiles + tile]
            for kk in range(owners):

                @pl.when(k == kk)
                def _():
                    out[t] = pieces[kk][slot]


def collect(meta, pieces, tiles):
    owners = len(pieces)
    slots, rows, width = pieces[0].shape
    return pl.pallas_call(
        functools.partial(collect_kernel, owners, slots, tiles),
        out_shape=[jax.ShapeDtypeStruct((tiles, rows, width), pieces[0].dtype)] * 2,
        in_specs=[pl.BlockSpec(memory_space=pltpu.SMEM)]
        + [pl.BlockSpec(memory_space=pltpu.VMEM)] * owners,
        out_specs=[pl.BlockSpec(memory_space=pltpu.VMEM)] * 2,
        compiler_params=pltpu.CompilerParams(vmem_limit_bytes=32 << 20),
        cost_estimate=pl.CostEstimate(
            flops=0, bytes_accessed=8 * tiles * rows * width, transcendentals=0
        ),
    )(meta, *pieces)


def shards(tokens, cotangent, w_up, w_down, active):
    owners = lax.axis_size("tensor")
    replicas = lax.axis_size("dp")
    subs = lax.axis_size("sub")
    if replicas != 2 or subs != 2 or active.shape[2] != 1 or tokens.shape[2] % 16:
        return plain(tokens, cotangent, w_up, w_down, active)
    tiles = tokens.shape[1]
    rows = tokens.shape[2]
    slots = MOST + replicas - 1
    side = lax.axis_index("dp")
    place = lax.axis_index("tensor")

    listed = active.reshape(tiles)
    listed_other = swap(jnp.broadcast_to(listed[None, :], (8, tiles)), "dp")[0]
    blocks = ordered(listed, listed_other, side, 0)
    tok_keep, tok_pass = halves(tokens[0], side)
    tok_got = swap(tok_pass, "dp")

    owner_ids = jnp.arange(owners, dtype=jnp.int32)
    hot = (blocks[:, None] == owner_ids[None, :]).astype(jnp.int32)
    counts = jnp.sum(hot, axis=0)
    before = (jnp.arange(2 * tiles)[None, :] < jnp.arange(2 * tiles)[:, None]) & (
        blocks[:, None] == blocks[None, :]
    )
    slot_of = jnp.sum(before.astype(jnp.int32), axis=1)
    match = (
        (blocks[None, None, :] == owner_ids[:, None, None])
        & (slot_of[None, None, :] == jnp.arange(slots, dtype=jnp.int32)[None, :, None])
    )
    table = jnp.sum(match * jnp.arange(2 * tiles, dtype=jnp.int32)[None, None, :], axis=2)
    meta = jnp.concatenate(
        [
            jnp.stack([side, place]).astype(jnp.int32),
            table.reshape(-1).astype(jnp.int32),
            blocks.astype(jnp.int32),
            slot_of.astype(jnp.int32),
        ]
    )
    crowd = jnp.max(counts)
    crowd = jnp.maximum(crowd, swap(jnp.broadcast_to(crowd, (8, 128)), "groups")[0, 0])
    mine_count = jnp.sum(jnp.where(owner_ids == place, counts, 0))

    def balanced(tok_keep, tok_got, cotangent, w_up, w_down, meta, mine_count):
        def send(keep, got):
            pieces = dispatch(meta, keep, got, owners, slots)
            arrived = [pieces[0]] + [
                lax.ppermute(pieces[k], "tensor", [(i, (i + k) % owners) for i in range(owners)])
                for k in range(1, owners)
            ]
            return jnp.concatenate(arrived, 0).reshape(owners * slots * rows, -1)

        def both_rows(w):
            keep, pass_on = halves(w, side)
            return ordered(keep, swap(pass_on, "dp"), side, 0)

        def total(part):
            part = part + swap(part.astype(BF16), "sub").astype(F32)
            return part + swap(part.astype(BF16), "dp").astype(F32)

        cot_keep, cot_pass = halves(cotangent[0], side)
        cot_got = swap(cot_pass, "dp")
        tok = send(tok_keep, tok_got)
        up = both_rows(w_up)
        down = both_rows(w_down)
        cot = send(cot_keep, cot_got)
        dims = (((1,), (1,)), ((), ()))
        hidden = total(lax.dot_general(tok, up, dims, preferred_element_type=F32))
        grad_act = total(lax.dot_general(cot, down, dims, preferred_element_type=F32))
        filled = (jnp.arange(slots) < mine_count)[None, :, None, None]
        filled = jnp.broadcast_to(filled, (owners, slots, rows, 1)).reshape(-1, 1)
        positive = jnp.where(filled, jnp.maximum(hidden, 0.0), 0.0)
        squared = (positive * positive).astype(BF16)
        grad_hidden = (2.0 * positive * grad_act).astype(BF16)
        back = jnp.dot(grad_hidden, up, preferred_element_type=F32).astype(BF16)
        back = back.reshape(owners, slots, rows, -1)
        home = [back[0]] + [
            lax.ppermute(back[k], "tensor", [((i + k) % owners, i) for i in range(owners)])
            for k in range(1, owners)
        ]
        mine, other = collect(meta, home, tiles)
        grad_tokens = ordered(mine, swap(other, "dp"), side, 2)[None]

        def weight_grad(act, data):
            g = lax.dot_general(act, data, (((0,), (0,)), ((), ())), preferred_element_type=F32).astype(BF16)
            n = g.shape[0] // 2
            keep = lax.dynamic_slice_in_dim(g, side * n, n, 0)
            pass_on = lax.dynamic_slice_in_dim(g, (1 - side) * n, n, 0)
            return ordered(keep, swap(pass_on, "dp"), side, 1)

        return grad_tokens, weight_grad(grad_hidden, tok), weight_grad(squared, cot)

    return lax.cond(
        crowd <= slots,
        lambda: balanced(tok_keep, tok_got, cotangent, w_up, w_down, meta, mine_count),
        lambda: plain(tokens, cotangent, w_up, w_down, active),
    )


def solution(mesh):
    placed = (
        P(("groups", "dp"), None, "tensor", "sub"),
        P(("groups", "dp"), None, "tensor", "sub"),
        P(("tensor", "dp"), "sub"),
        P(("tensor", "dp"), "sub"),
        P(("groups", "dp"), None, None),
    )
    return jax.shard_map(
        shards,
        mesh=mesh,
        in_specs=placed,
        out_specs=(
            P(("groups", "dp"), None, "tensor", "sub"),
            P(("groups", "tensor", "dp"), "sub"),
            P(("groups", "tensor", "dp"), "sub"),
        ),
        check_vma=False,
    )
```

```python
import functools

import jax
import jax.numpy as jnp
from jax import lax
from jax.experimental import pallas as pl
from jax.experimental.pallas import tpu as pltpu
from jax.sharding import PartitionSpec as P

MOST = 3
EVEN = 2
EXTRA = 2
BY_SLOT = 6
SLOTS = 2 * MOST
F32 = jnp.float32
BF16 = jnp.bfloat16


def swap(x, axis):
    return lax.ppermute(x, axis, [(0, 1), (1, 0)])


def ordered(mine, other, side, axis):
    return jnp.where(
        side == 0,
        jnp.concatenate([mine, other], axis),
        jnp.concatenate([other, mine], axis),
    )


def all_rows(w):
    if lax.axis_size("dp") != 2:
        return lax.all_gather(w, "dp", axis=0, tiled=True)
    return ordered(w, swap(w, "dp"), lax.axis_index("dp"), 0)


def sub_total(part):
    if lax.axis_size("sub") != 2:
        return lax.psum(part.astype(BF16), "sub").astype(F32)
    rounded = part.astype(BF16)
    return rounded.astype(F32) + swap(rounded, "sub").astype(F32)


def replica_total(part):
    if lax.axis_size("dp") != 2:
        return lax.psum_scatter(part.astype(BF16), "dp", scatter_dimension=0, tiled=True)
    side = lax.axis_index("dp")
    n = part.shape[0] // 2
    rounded = part.astype(BF16)
    keep = lax.dynamic_slice_in_dim(rounded, side * n, n, 0)
    pass_on = lax.dynamic_slice_in_dim(rounded, (1 - side) * n, n, 0)
    return (keep.astype(F32) + swap(pass_on, "dp").astype(F32)).astype(BF16)


def plain(tokens, cotangent, w_up, w_down, active):
    tile_count = tokens.shape[1]
    part_rows = tokens.shape[2]
    half_width = tokens.shape[3]
    owners = lax.axis_size("tensor")
    block_ids = active[0]
    owner_list = jnp.arange(owners, dtype=jnp.int32)
    listed = jnp.any(block_ids[:, :, None] == owner_list[None, None, :], axis=1).astype(jnp.int32)
    ranking = jnp.cumsum(listed, axis=0) - 1
    slot_ids = jnp.arange(MOST, dtype=jnp.int32)
    choose = (listed.T[:, None, :] == 1) & (ranking.T[:, None, :] == slot_ids[None, :, None])
    choose_half = choose.astype(BF16)
    choose_full = choose.astype(F32)
    send_tok = jnp.einsum("omt,trd->omrd", choose_half, tokens[0], preferred_element_type=F32).astype(BF16)
    send_cot = jnp.einsum("omt,trd->omrd", choose_half, cotangent[0], preferred_element_type=F32).astype(BF16)
    up_weight_block = all_rows(w_up)
    down_weight_block = all_rows(w_down)
    slot_token = lax.all_to_all(send_tok, "tensor", split_axis=0, concat_axis=2, tiled=True)[0]
    slot_cotangent = lax.all_to_all(send_cot, "tensor", split_axis=0, concat_axis=2, tiled=True)[0]
    hidden = sub_total(jnp.einsum("bkn,vn->bkv", slot_token, up_weight_block, preferred_element_type=F32))
    grad_act = sub_total(jnp.einsum("bkn,vn->bkv", slot_cotangent, down_weight_block, preferred_element_type=F32))
    positive = jnp.maximum(hidden, 0.0)
    squared_activation = (positive * positive).astype(BF16)
    hidden_gradient = (2.0 * positive * grad_act).astype(BF16)
    back_rows = jnp.einsum("opl,la->opa", hidden_gradient, up_weight_block, preferred_element_type=F32).astype(BF16)
    back_rows = back_rows.reshape(MOST, owners, part_rows, half_width)
    received = lax.all_to_all(back_rows, "tensor", split_axis=1, concat_axis=1, tiled=True)
    summed = jnp.einsum("omt,mord->trd", choose_full, received.astype(F32), precision=lax.Precision.HIGHEST)
    grad_tokens = summed.astype(BF16).reshape(1, tile_count, part_rows, half_width)
    up_weight_term = jnp.einsum("epn,epk->nk", hidden_gradient, slot_token, preferred_element_type=F32)
    down_weight_term = jnp.einsum("epn,epk->nk", squared_activation, slot_cotangent, preferred_element_type=F32)
    return grad_tokens, replica_total(up_weight_term), replica_total(down_weight_term)


def after(x, *first):
    return lax.optimization_barrier((x, first))[0]


def halves(x, side):
    width = x.shape[-1] // 2
    keep = lax.dynamic_slice_in_dim(x, side * width, width, x.ndim - 1)
    pass_on = lax.dynamic_slice_in_dim(x, (1 - side) * width, width, x.ndim - 1)
    return keep, pass_on


def copy_rows(src, at, dst, to, start=0):
    step = 512

    @pl.loop(0, dst.shape[-1] // step)
    def _(i):
        cols = pl.ds(pl.multiple_of(i * step, step), step)
        dst[to, :, cols] = src[at, :, pl.ds(pl.multiple_of(start + i * step, step), step)]


def plan_kernel(owners, tiles, mine, other, out):
    side, place = lax.axis_index("dp"), lax.axis_index("tensor")
    block = [jnp.where(side == i // tiles, mine[i % tiles], other[i % tiles]) for i in range(2 * tiles)]
    low = [sum((b == o).astype(jnp.int32) for b in block[:tiles]) for o in range(owners)]
    high = [sum((b == o).astype(jnp.int32) for b in block[tiles:]) for o in range(owners)]
    crowded, most = jnp.int32(0), low[0] + high[0]
    for o in range(1, owners):
        more = low[o] + high[o] > most
        crowded, most = jnp.where(more, o, crowded), jnp.where(more, low[o] + high[o], most)
    fits, mine_count, mine_first, first = most <= EVEN + EXTRA, 0, 0, []
    for o in range(owners):
        count = low[o] + high[o]
        fits = fits & ((o == crowded) | (count <= 1) | ((low[o] == 1) & (high[o] == 1)))
        last = jnp.where(o == crowded, EVEN + EXTRA, EVEN) - 1
        local = jnp.where(side == 0, low[o], high[o])
        first.append(jnp.minimum(jnp.where(local > 0, jnp.where(side == 0, 0, low[o]), last), last))
        mine_count = jnp.where(place == o, count, mine_count)
        mine_first = jnp.where(place == o, first[o], mine_first)
    head = (side, place, crowded, mine_count, mine_first, jnp.where(fits, crowded, owners))
    for i, value in enumerate(head):
        out[i] = value
    by_position, by_tile = BY_SLOT + owners * SLOTS, BY_SLOT + 2 * owners * SLOTS
    for i in range(BY_SLOT, by_tile):
        out[i] = 0
    for i, b in enumerate(block):
        slot = jnp.minimum(sum([(b == c).astype(jnp.int32) for c in block[:i]], jnp.int32(0)), SLOTS - 1)
        start = sum(jnp.where(b == o, first[o], 0) for o in range(owners))
        position = jnp.where(slot == start, 0, jnp.where(slot < start, slot + 1, slot))
        out[BY_SLOT + b * SLOTS + slot] = i
        out[by_position + b * SLOTS + position] = i
        out[by_tile + i] = b
        out[by_tile + 2 * tiles + i] = slot


def plan(mine, other, owners, tiles):
    smem = pl.BlockSpec(memory_space=pltpu.SMEM)
    return pl.pallas_call(
        functools.partial(plan_kernel, owners, tiles),
        out_shape=jax.ShapeDtypeStruct((BY_SLOT + 2 * owners * SLOTS + 4 * tiles,), jnp.int32),
        in_specs=[smem, smem],
        out_specs=smem,
    )(mine, other)


def call(kernel, out_shape, n_vmem, scratch=(), flops=0, moved=0):
    vmem = pl.BlockSpec(memory_space=pltpu.VMEM)
    return pl.pallas_call(
        kernel,
        out_shape=out_shape,
        in_specs=[pl.BlockSpec(memory_space=pltpu.SMEM)] + [vmem] * n_vmem,
        out_specs=[vmem] * len(out_shape),
        scratch_shapes=list(scratch),
        compiler_params=pltpu.CompilerParams(vmem_limit_bytes=40 << 20),
        cost_estimate=pl.CostEstimate(flops=flops, bytes_accessed=moved, transcendentals=0),
    )


def dispatch_kernel(owners, tiles, base, groups, meta, keep, got, *outs):
    side, place, crowded = meta[0], meta[1], meta[2]
    n = 0
    for first, count, each in groups:
        for k in range(owners if each else 1):
            owner = lax.rem(place + k, owners) if each else crowded
            out = outs[n]

            @pl.loop(0, count)
            def _(s):
                tile = meta[base + owner * SLOTS + first + s]
                own = lax.div(tile, tiles) == side
                at = lax.rem(tile, tiles)

                @pl.when(own)
                def _():
                    copy_rows(keep, at, out, s, side * out.shape[2])

                @pl.when(jnp.logical_not(own))
                def _():
                    copy_rows(got, at, out, s)

            n += 1


def dispatch(meta, keep, got, owners, base, groups):
    tiles, rows, width = got.shape
    counts = [count for _, count, each in groups for _ in range(owners if each else 1)]
    outs = [jax.ShapeDtypeStruct((c, rows, width), got.dtype) for c in counts]
    kernel = functools.partial(dispatch_kernel, owners, tiles, base, groups)
    return call(kernel, outs, 2, moved=4 * sum(counts) * rows * width)(meta, keep, got)


def first_kernel(owners, tiles, listed, keep, *outs):
    side, place = lax.axis_index("dp"), lax.axis_index("tensor")
    for k in range(owners):
        owner = lax.rem(place + k, owners)
        at = jnp.int32(0)
        for t in reversed(range(tiles)):
            at = jnp.where(listed[t] == owner, t, at)
        copy_rows(keep, at, outs[k], 0, side * outs[k].shape[2])


def rows_of(pieces, counts, owners, cols):
    parts, n = [], 0
    for count in counts:
        for s in range(count):
            parts += [pieces[n + k][s, :, cols] for k in range(owners)]
        n += owners
    return jnp.concatenate(parts, 0)


def product_kernel(counts, owners, moved, meta, *rest):
    pieces, weight, out, total = rest[:-3], rest[-3], rest[-2], rest[-1]
    step = 512
    total[...] = jnp.zeros_like(total)

    @pl.loop(0, weight.shape[1] // step)
    def _(i):
        cols = pl.ds(pl.multiple_of(i * step, step), step)
        total[...] += lax.dot_general(
            rows_of(pieces, counts, owners, cols),
            weight[:, cols],
            (((1,), (1,)), ((), ())),
            preferred_element_type=F32,
        )

    n = out.shape[1]
    for p in range(sum(counts)):
        out[slot_at(meta[4], p) if moved else p] = total[p * n : (p + 1) * n].astype(BF16)


def slot_at(first, p):
    return first if p == 0 else jnp.where(p <= first, p - 1, p)


def product(meta, groups, weight, moved):
    owners = len(groups[0])
    counts = [g[0].shape[0] for g in groups]
    pieces = [p for g in groups for p in g]
    n, m, rows = sum(counts), weight.shape[0], pieces[0].shape[1] * owners
    return call(
        functools.partial(product_kernel, counts, owners, moved),
        [jax.ShapeDtypeStruct((n, rows, m), BF16)],
        len(pieces) + 1,
        [pltpu.VMEM((n * rows, m), F32)],
        flops=2 * n * rows * m * weight.shape[1],
        moved=2 * (n * rows + m) * weight.shape[1],
    )(meta, *pieces, weight)[0]


def squared_kernel(meta, h1, h2, positive, squared):
    for s in range(h1.shape[0]):
        h = jnp.maximum(h1[s].astype(F32) + h2[s].astype(F32), 0.0)
        h = jnp.where(s < meta[3], h, 0.0)
        positive[s] = h
        squared[s] = (h * h).astype(BF16)


def back_kernel(first, count, owners, meta, positive, g1, g2, up, grad_hidden, *outs):
    n, m = g1.shape[1], g1.shape[2]
    rows = n // owners
    for s in range(count):
        grad_act = g1[s].astype(F32) + g2[s].astype(F32)
        grad_hidden[s] = (2.0 * positive[first + s] * grad_act).astype(BF16)
    step = 512

    @pl.loop(0, up.shape[1] // step)
    def _(i):
        cols = pl.ds(pl.multiple_of(i * step, step), step)
        out = jnp.dot(
            grad_hidden[...].reshape(count * n, m), up[:, cols], preferred_element_type=F32
        ).astype(BF16)
        for s in range(count):
            for k in range(owners):
                at = s * n + k * rows
                outs[k][s, :, cols] = out[at : at + rows]


def back(meta, positive, g, up, first, owners):
    count, n, m = g[0].shape
    width = up.shape[1]
    outs = call(
        functools.partial(back_kernel, first, count, owners),
        [jax.ShapeDtypeStruct((count, n, m), BF16)]
        + [jax.ShapeDtypeStruct((count, n // owners, width), BF16)] * owners,
        4,
        flops=2 * count * n * m * width,
        moved=2 * (count * n + m) * width,
    )(meta, positive, *g, up)
    return outs[0], list(outs[1:])


def weights_kernel(owners, act_counts, counts, moved, meta, *rest):
    acts, data, rest = rest[: len(act_counts)], rest[len(act_counts) : -4], rest[-4:]
    keep, pass_on, by_slot, turned = rest
    side = meta[0]
    n, m = acts[0].shape[1], acts[0].shape[2]
    p = 0
    for act, count in zip(acts, act_counts):
        by_slot[p : p + count] = act[...]
        p += count
    for p in range(sum(counts)):
        turned[:, p * n : (p + 1) * n] = by_slot[slot_at(meta[4], p) if moved else p].T
    step = 256

    @pl.loop(0, keep.shape[1] // step)
    def _(i):
        cols = pl.ds(pl.multiple_of(i * step, step), step)
        g = jnp.dot(turned[...], rows_of(data, counts, owners, cols), preferred_element_type=F32)
        low, high = g[: m // 2].astype(BF16), g[m // 2 :].astype(BF16)
        keep[:, cols] = jnp.where(side == 0, low, high)
        pass_on[:, cols] = jnp.where(side == 0, high, low)


def weights(meta, acts, groups, moved):
    owners = len(groups[0])
    act_counts, counts = [a.shape[0] for a in acts], [g[0].shape[0] for g in groups]
    data = [p for g in groups for p in g]
    _, n, m = acts[0].shape
    slots, width = sum(counts), data[0].shape[2]
    return call(
        functools.partial(weights_kernel, owners, act_counts, counts, moved),
        [jax.ShapeDtypeStruct((m // 2, width), BF16)] * 2,
        len(acts) + len(data),
        [pltpu.VMEM((slots, n, m), BF16), pltpu.VMEM((m, slots * n), BF16)],
        flops=2 * slots * n * m * width,
        moved=2 * (slots * n + m) * width,
    )(meta, *acts, *data)


def collect_kernel(owners, tiles, base, meta, *rest):
    pieces, (mine, other) = rest[:-2], rest[-2:]
    side, place = meta[0], meta[1]
    even = pieces[0].shape[0]
    for r, out in enumerate((mine, other)):
        replica = side if r == 0 else 1 - side

        @pl.loop(0, tiles)
        def _(t):
            tile = replica * tiles + t
            k = lax.rem(meta[base + tile] - place + owners, owners)
            slot = meta[base + 2 * tiles + tile]
            for kk in range(owners):

                @pl.when((k == kk) & (slot < even))
                def _():
                    copy_rows(pieces[kk], slot, out, t)

                if len(pieces) > owners:

                    @pl.when((k == kk) & (slot >= even))
                    def _():
                        copy_rows(pieces[owners + kk], slot - even, out, t)


def collect(meta, pieces, tiles, owners, base):
    _, rows, width = pieces[0].shape
    kernel = functools.partial(collect_kernel, owners, tiles, base)
    outs = [jax.ShapeDtypeStruct((tiles, rows, width), BF16)] * 2
    return call(kernel, outs, len(pieces), moved=8 * tiles * rows * width)(meta, *pieces)


def shards(tokens, cotangent, w_up, w_down, active):
    owners = lax.axis_size("tensor")
    replicas = lax.axis_size("dp")
    subs = lax.axis_size("sub")
    if replicas != 2 or subs != 2 or active.shape[2] != 1 or tokens.shape[2] % 16:
        return plain(tokens, cotangent, w_up, w_down, active)
    tiles = tokens.shape[1]
    rows = tokens.shape[2]
    side = lax.axis_index("dp")
    place = lax.axis_index("tensor")
    def forth(k):
        return [(i, (i + k) % owners) for i in range(owners)]

    def back_of(pairs):
        return [(b, a) for a, b in pairs]

    def move(pieces, perm_of):
        return [pieces[0]] + [lax.ppermute(pieces[k], "tensor", perm_of(k)) for k in range(1, owners)]

    def other_half(x):
        width = x.shape[-1] // 2
        return lax.dynamic_slice_in_dim(x, (1 - side) * width, width, x.ndim - 1)

    tok_pass = other_half(tokens[0])
    listed_other = swap(after(active, tok_pass), "dp").reshape(tiles)
    tok_got = swap(tok_pass, "dp")
    listed = active.reshape(tiles)
    one = jax.ShapeDtypeStruct((1,) + tok_pass.shape[1:], BF16)
    first = functools.partial(first_kernel, owners, tiles)
    tok_first = move(call(first, [one] * owners, 1, moved=2 * tok_pass.size)(listed, tokens[0]), forth)
    meta = plan(listed, listed_other, owners, tiles)
    by_slot = BY_SLOT
    by_position = by_slot + owners * SLOTS
    by_tile = by_position + owners * SLOTS
    cot_pass = other_half(cotangent[0])
    up_keep, up_pass = halves(w_up, side)
    down_keep, down_pass = halves(w_down, side)
    extra_group = (EVEN, EXTRA, False)
    tok_sent = dispatch(meta, tokens[0], tok_got, owners, by_position, ((1, EVEN - 1, True), extra_group))

    def run(center=None):
        fast = center is not None

        def extra_forth(k):
            return [((center - k) % owners, center)]

        def over_subs(part):
            return (part.astype(F32) + swap(part, "sub").astype(F32)).astype(BF16)

        cot_got = swap(cot_pass, "dp")
        if fast:
            tok = [tok_first, move(tok_sent[:owners], forth), move([tok_sent[owners]] * owners, extra_forth)]
            cot_groups = ((0, EVEN, True), extra_group)
            cot_sent = dispatch(meta, cotangent[0], cot_got, owners, by_slot, cot_groups)
            cot = [move(cot_sent[:owners], forth), move([cot_sent[owners]] * owners, extra_forth)]
        else:
            cot_groups = ((0, SLOTS, True),)
            tok, cot = [
                [move(dispatch(meta, keep, got, owners, by_slot, cot_groups), forth)]
                for keep, got in ((tokens[0], tok_got), (cotangent[0], cot_got))
            ]
        up = ordered(up_keep, swap(up_pass, "dp"), side, 0)
        down = ordered(down_keep, swap(down_pass, "dp"), side, 0)
        hidden = over_subs(product(meta, tok, up, fast))
        shape = hidden.shape
        positive, squared = call(
            squared_kernel,
            [jax.ShapeDtypeStruct(shape, F32), jax.ShapeDtypeStruct(shape, BF16)],
            2,
            moved=8 * hidden.size,
        )(meta, hidden, swap(hidden, "dp"))
        grad_hidden, home = [None] * len(cot), [None] * len(cot)
        for i in reversed(range(len(cot))):
            first, _, each = cot_groups[i]
            grad_act = over_subs(product(meta, [cot[i]], down, False))
            sums = (grad_act, swap(grad_act, "dp"))
            grad_hidden[i], out = back(meta, positive, sums, up, first, owners)
            perm_of = forth if each else extra_forth
            home[i] = move(out, lambda k: back_of(perm_of(k)))
            down = after(down, grad_hidden[i])
        down_grad, down_other = weights(meta, [squared], cot, False)
        down_got = swap(after(down_other, sums[1]), "dp")
        up_grad, up_other = weights(meta, grad_hidden, tok, fast)
        up_got = swap(up_other, "dp")
        home = [piece for group in home for piece in group]
        mine, other = collect(meta, home, tiles, owners, by_tile)
        return (
            ordered(mine, swap(other, "dp"), side, 2)[None],
            ordered(up_grad, up_got, side, 1),
            ordered(down_grad, down_got, side, 1),
        )

    return lax.switch(
        meta[5],
        [functools.partial(run, center) for center in range(owners)] + [run],
    )


def solution(mesh):
    placed = (
        P(("groups", "dp"), None, "tensor", "sub"),
        P(("groups", "dp"), None, "tensor", "sub"),
        P(("tensor", "dp"), "sub"),
        P(("tensor", "dp"), "sub"),
        P(("groups", "dp"), None, None),
    )
    return jax.shard_map(
        shards,
        mesh=mesh,
        in_specs=placed,
        out_specs=(
            P(("groups", "dp"), None, "tensor", "sub"),
            P(("groups", "tensor", "dp"), "sub"),
            P(("groups", "tensor", "dp"), "sub"),
        ),
        check_vma=False,
    )
```

```python
import functools

import jax
import jax.numpy as jnp
from jax import lax
from jax.experimental import pallas as pl
from jax.experimental.pallas import tpu as pltpu
from jax.sharding import PartitionSpec as P

MOST = 3
EVEN = 2
EXTRA = 2
BY_SLOT = 6
SLOTS = 2 * MOST
F32 = jnp.float32
BF16 = jnp.bfloat16


def swap(x, axis):
    return lax.ppermute(x, axis, [(0, 1), (1, 0)])


def ordered(mine, other, side, axis):
    return jnp.where(
        side == 0,
        jnp.concatenate([mine, other], axis),
        jnp.concatenate([other, mine], axis),
    )


def all_rows(w):
    if lax.axis_size("dp") != 2:
        return lax.all_gather(w, "dp", axis=0, tiled=True)
    return ordered(w, swap(w, "dp"), lax.axis_index("dp"), 0)


def sub_total(part):
    if lax.axis_size("sub") != 2:
        return lax.psum(part.astype(BF16), "sub").astype(F32)
    rounded = part.astype(BF16)
    return rounded.astype(F32) + swap(rounded, "sub").astype(F32)


def replica_total(part):
    if lax.axis_size("dp") != 2:
        return lax.psum_scatter(part.astype(BF16), "dp", scatter_dimension=0, tiled=True)
    side = lax.axis_index("dp")
    n = part.shape[0] // 2
    rounded = part.astype(BF16)
    keep = lax.dynamic_slice_in_dim(rounded, side * n, n, 0)
    pass_on = lax.dynamic_slice_in_dim(rounded, (1 - side) * n, n, 0)
    return (keep.astype(F32) + swap(pass_on, "dp").astype(F32)).astype(BF16)


def plain(tokens, cotangent, w_up, w_down, active):
    tile_count = tokens.shape[1]
    part_rows = tokens.shape[2]
    half_width = tokens.shape[3]
    owners = lax.axis_size("tensor")
    block_ids = active[0]
    owner_list = jnp.arange(owners, dtype=jnp.int32)
    listed = jnp.any(block_ids[:, :, None] == owner_list[None, None, :], axis=1).astype(jnp.int32)
    ranking = jnp.cumsum(listed, axis=0) - 1
    slot_ids = jnp.arange(MOST, dtype=jnp.int32)
    choose = (listed.T[:, None, :] == 1) & (ranking.T[:, None, :] == slot_ids[None, :, None])
    choose_half = choose.astype(BF16)
    choose_full = choose.astype(F32)
    send_tok = jnp.einsum("omt,trd->omrd", choose_half, tokens[0], preferred_element_type=F32).astype(BF16)
    send_cot = jnp.einsum("omt,trd->omrd", choose_half, cotangent[0], preferred_element_type=F32).astype(BF16)
    up_weight_block = all_rows(w_up)
    down_weight_block = all_rows(w_down)
    slot_token = lax.all_to_all(send_tok, "tensor", split_axis=0, concat_axis=2, tiled=True)[0]
    slot_cotangent = lax.all_to_all(send_cot, "tensor", split_axis=0, concat_axis=2, tiled=True)[0]
    hidden = sub_total(jnp.einsum("bkn,vn->bkv", slot_token, up_weight_block, preferred_element_type=F32))
    grad_act = sub_total(jnp.einsum("bkn,vn->bkv", slot_cotangent, down_weight_block, preferred_element_type=F32))
    positive = jnp.maximum(hidden, 0.0)
    squared_activation = (positive * positive).astype(BF16)
    hidden_gradient = (2.0 * positive * grad_act).astype(BF16)
    back_rows = jnp.einsum("opl,la->opa", hidden_gradient, up_weight_block, preferred_element_type=F32).astype(BF16)
    back_rows = back_rows.reshape(MOST, owners, part_rows, half_width)
    received = lax.all_to_all(back_rows, "tensor", split_axis=1, concat_axis=1, tiled=True)
    summed = jnp.einsum("omt,mord->trd", choose_full, received.astype(F32), precision=lax.Precision.HIGHEST)
    grad_tokens = summed.astype(BF16).reshape(1, tile_count, part_rows, half_width)
    up_weight_term = jnp.einsum("epn,epk->nk", hidden_gradient, slot_token, preferred_element_type=F32)
    down_weight_term = jnp.einsum("epn,epk->nk", squared_activation, slot_cotangent, preferred_element_type=F32)
    return grad_tokens, replica_total(up_weight_term), replica_total(down_weight_term)


def after(x, *first):
    return lax.optimization_barrier((x, first))[0]


def halves(x, side):
    width = x.shape[-1] // 2
    keep = lax.dynamic_slice_in_dim(x, side * width, width, x.ndim - 1)
    pass_on = lax.dynamic_slice_in_dim(x, (1 - side) * width, width, x.ndim - 1)
    return keep, pass_on


def copy_rows(src, at, dst, to, start=0):
    step = 512

    @pl.loop(0, dst.shape[-1] // step)
    def _(i):
        cols = pl.ds(pl.multiple_of(i * step, step), step)
        dst[to, :, cols] = src[at, :, pl.ds(pl.multiple_of(start + i * step, step), step)]


def plan_kernel(owners, tiles, mine, other, out):
    side, place = lax.axis_index("dp"), lax.axis_index("tensor")
    block = [jnp.where(side == i // tiles, mine[i % tiles], other[i % tiles]) for i in range(2 * tiles)]
    low = [sum((b == o).astype(jnp.int32) for b in block[:tiles]) for o in range(owners)]
    high = [sum((b == o).astype(jnp.int32) for b in block[tiles:]) for o in range(owners)]
    crowded, most = jnp.int32(0), low[0] + high[0]
    for o in range(1, owners):
        more = low[o] + high[o] > most
        crowded, most = jnp.where(more, o, crowded), jnp.where(more, low[o] + high[o], most)
    fits, mine_count, mine_first, first = most <= EVEN + EXTRA, 0, 0, []
    for o in range(owners):
        count = low[o] + high[o]
        fits = fits & ((o == crowded) | (count <= 1) | ((low[o] == 1) & (high[o] == 1)))
        last = jnp.where(o == crowded, EVEN + EXTRA, EVEN) - 1
        local = jnp.where(side == 0, low[o], high[o])
        first.append(jnp.minimum(jnp.where(local > 0, jnp.where(side == 0, 0, low[o]), last), last))
        mine_count = jnp.where(place == o, count, mine_count)
        mine_first = jnp.where(place == o, first[o], mine_first)
    head = (side, place, crowded, mine_count, mine_first, jnp.where(fits, crowded, owners))
    for i, value in enumerate(head):
        out[i] = value
    by_position, by_tile = BY_SLOT + owners * SLOTS, BY_SLOT + 2 * owners * SLOTS
    for i in range(BY_SLOT, by_tile):
        out[i] = 0
    for i, b in enumerate(block):
        slot = jnp.minimum(sum([(b == c).astype(jnp.int32) for c in block[:i]], jnp.int32(0)), SLOTS - 1)
        start = sum(jnp.where(b == o, first[o], 0) for o in range(owners))
        position = jnp.where(slot == start, 0, jnp.where(slot < start, slot + 1, slot))
        out[BY_SLOT + b * SLOTS + slot] = i
        out[by_position + b * SLOTS + position] = i
        out[by_tile + i] = b
        out[by_tile + 2 * tiles + i] = slot


def plan(mine, other, owners, tiles):
    smem = pl.BlockSpec(memory_space=pltpu.SMEM)
    return pl.pallas_call(
        functools.partial(plan_kernel, owners, tiles),
        out_shape=jax.ShapeDtypeStruct((BY_SLOT + 2 * owners * SLOTS + 4 * tiles,), jnp.int32),
        in_specs=[smem, smem],
        out_specs=smem,
    )(mine, other)


def call(kernel, out_shape, n_vmem, scratch=(), flops=0, moved=0):
    vmem = pl.BlockSpec(memory_space=pltpu.VMEM)
    return pl.pallas_call(
        kernel,
        out_shape=out_shape,
        in_specs=[pl.BlockSpec(memory_space=pltpu.SMEM)] + [vmem] * n_vmem,
        out_specs=[vmem] * len(out_shape),
        scratch_shapes=list(scratch),
        compiler_params=pltpu.CompilerParams(vmem_limit_bytes=40 << 20),
        cost_estimate=pl.CostEstimate(flops=flops, bytes_accessed=moved, transcendentals=0),
    )


def dispatch_kernel(owners, tiles, base, groups, meta, keep, got, *outs):
    side, place, crowded = meta[0], meta[1], meta[2]
    n = 0
    for first, count, each in groups:
        for k in range(owners if each else 1):
            owner = lax.rem(place + k, owners) if each else crowded
            out = outs[n]

            @pl.loop(0, count)
            def _(s):
                tile = meta[base + owner * SLOTS + first + s]
                own = lax.div(tile, tiles) == side
                at = lax.rem(tile, tiles)

                @pl.when(own)
                def _():
                    copy_rows(keep, at, out, s, side * out.shape[2])

                @pl.when(jnp.logical_not(own))
                def _():
                    copy_rows(got, at, out, s)

            n += 1


def dispatch(meta, keep, got, owners, base, groups):
    tiles, rows, width = got.shape
    counts = [count for _, count, each in groups for _ in range(owners if each else 1)]
    outs = [jax.ShapeDtypeStruct((c, rows, width), got.dtype) for c in counts]
    kernel = functools.partial(dispatch_kernel, owners, tiles, base, groups)
    return call(kernel, outs, 2, moved=4 * sum(counts) * rows * width)(meta, keep, got)


def first_kernel(owners, tiles, listed, keep, *outs):
    side, place = lax.axis_index("dp"), lax.axis_index("tensor")
    for k in range(owners):
        owner = lax.rem(place + k, owners)
        at = jnp.int32(0)
        for t in reversed(range(tiles)):
            at = jnp.where(listed[t] == owner, t, at)
        copy_rows(keep, at, outs[k], 0, side * outs[k].shape[2])


def rows_of(pieces, counts, owners, cols):
    parts, n = [], 0
    for count in counts:
        for s in range(count):
            parts += [pieces[n + k][s, :, cols] for k in range(owners)]
        n += owners
    return jnp.concatenate(parts, 0)


def product_kernel(counts, owners, moved, meta, *rest):
    pieces, weight, out, total = rest[:-3], rest[-3], rest[-2], rest[-1]
    step = 512
    total[...] = jnp.zeros_like(total)

    @pl.loop(0, weight.shape[1] // step)
    def _(i):
        cols = pl.ds(pl.multiple_of(i * step, step), step)
        total[...] += lax.dot_general(
            rows_of(pieces, counts, owners, cols),
            weight[:, cols],
            (((1,), (1,)), ((), ())),
            preferred_element_type=F32,
        )

    n = out.shape[1]
    for p in range(sum(counts)):
        out[slot_at(meta[4], p) if moved else p] = total[p * n : (p + 1) * n].astype(BF16)


def slot_at(first, p):
    return first if p == 0 else jnp.where(p <= first, p - 1, p)


def product(meta, groups, weight, moved):
    owners = len(groups[0])
    counts = [g[0].shape[0] for g in groups]
    pieces = [p for g in groups for p in g]
    n, m, rows = sum(counts), weight.shape[0], pieces[0].shape[1] * owners
    return call(
        functools.partial(product_kernel, counts, owners, moved),
        [jax.ShapeDtypeStruct((n, rows, m), BF16)],
        len(pieces) + 1,
        [pltpu.VMEM((n * rows, m), F32)],
        flops=2 * n * rows * m * weight.shape[1],
        moved=2 * (n * rows + m) * weight.shape[1],
    )(meta, *pieces, weight)[0]


def squared_kernel(meta, h1, h2, positive, squared):
    for s in range(h1.shape[0]):
        h = jnp.maximum(h1[s].astype(F32) + h2[s].astype(F32), 0.0)
        h = jnp.where(s < meta[3], h, 0.0)
        positive[s] = h
        squared[s] = (h * h).astype(BF16)


def back_kernel(first, count, owners, meta, positive, g1, g2, up, grad_hidden, *outs):
    n, m = g1.shape[1], g1.shape[2]
    rows = n // owners
    for s in range(count):
        grad_act = g1[s].astype(F32) + g2[s].astype(F32)
        grad_hidden[s] = (2.0 * positive[first + s] * grad_act).astype(BF16)
    step = 512

    @pl.loop(0, up.shape[1] // step)
    def _(i):
        cols = pl.ds(pl.multiple_of(i * step, step), step)
        out = jnp.dot(
            grad_hidden[...].reshape(count * n, m), up[:, cols], preferred_element_type=F32
        ).astype(BF16)
        for s in range(count):
            for k in range(owners):
                at = s * n + k * rows
                outs[k][s, :, cols] = out[at : at + rows]


def back(meta, positive, g, up, first, owners):
    count, n, m = g[0].shape
    width = up.shape[1]
    outs = call(
        functools.partial(back_kernel, first, count, owners),
        [jax.ShapeDtypeStruct((count, n, m), BF16)]
        + [jax.ShapeDtypeStruct((count, n // owners, width), BF16)] * owners,
        4,
        flops=2 * count * n * m * width,
        moved=2 * (count * n + m) * width,
    )(meta, positive, *g, up)
    return outs[0], list(outs[1:])


def weights_kernel(owners, act_counts, counts, moved, meta, *rest):
    acts, data, rest = rest[: len(act_counts)], rest[len(act_counts) : -4], rest[-4:]
    keep, pass_on, by_slot, turned = rest
    side = meta[0]
    n, m = acts[0].shape[1], acts[0].shape[2]
    p = 0
    for act, count in zip(acts, act_counts):
        by_slot[p : p + count] = act[...]
        p += count
    for p in range(sum(counts)):
        turned[:, p * n : (p + 1) * n] = by_slot[slot_at(meta[4], p) if moved else p].T
    step = 256

    @pl.loop(0, keep.shape[1] // step)
    def _(i):
        cols = pl.ds(pl.multiple_of(i * step, step), step)
        g = jnp.dot(turned[...], rows_of(data, counts, owners, cols), preferred_element_type=F32)
        low, high = g[: m // 2].astype(BF16), g[m // 2 :].astype(BF16)
        keep[:, cols] = jnp.where(side == 0, low, high)
        pass_on[:, cols] = jnp.where(side == 0, high, low)


def weights(meta, acts, groups, moved):
    owners = len(groups[0])
    act_counts, counts = [a.shape[0] for a in acts], [g[0].shape[0] for g in groups]
    data = [p for g in groups for p in g]
    _, n, m = acts[0].shape
    slots, width = sum(counts), data[0].shape[2]
    return call(
        functools.partial(weights_kernel, owners, act_counts, counts, moved),
        [jax.ShapeDtypeStruct((m // 2, width), BF16)] * 2,
        len(acts) + len(data),
        [pltpu.VMEM((slots, n, m), BF16), pltpu.VMEM((m, slots * n), BF16)],
        flops=2 * slots * n * m * width,
        moved=2 * (slots * n + m) * width,
    )(meta, *acts, *data)


def collect_kernel(owners, tiles, base, meta, *rest):
    pieces, (mine, other) = rest[:-2], rest[-2:]
    side, place = meta[0], meta[1]
    even = pieces[0].shape[0]
    for r, out in enumerate((mine, other)):
        replica = side if r == 0 else 1 - side

        @pl.loop(0, tiles)
        def _(t):
            tile = replica * tiles + t
            k = lax.rem(meta[base + tile] - place + owners, owners)
            slot = meta[base + 2 * tiles + tile]
            for kk in range(owners):

                @pl.when((k == kk) & (slot < even))
                def _():
                    copy_rows(pieces[kk], slot, out, t)

                if len(pieces) > owners:

                    @pl.when((k == kk) & (slot >= even))
                    def _():
                        copy_rows(pieces[owners + kk], slot - even, out, t)


def collect(meta, pieces, tiles, owners, base):
    _, rows, width = pieces[0].shape
    kernel = functools.partial(collect_kernel, owners, tiles, base)
    outs = [jax.ShapeDtypeStruct((tiles, rows, width), BF16)] * 2
    return call(kernel, outs, len(pieces), moved=8 * tiles * rows * width)(meta, *pieces)


def shards(tokens, cotangent, w_up, w_down, active):
    owners = lax.axis_size("tensor")
    replicas = lax.axis_size("dp")
    subs = lax.axis_size("sub")
    if replicas != 2 or subs != 2 or active.shape[2] != 1 or tokens.shape[2] % 16:
        return plain(tokens, cotangent, w_up, w_down, active)
    tiles = tokens.shape[1]
    rows = tokens.shape[2]
    side = lax.axis_index("dp")
    place = lax.axis_index("tensor")
    def forth(k):
        return [(i, (i + k) % owners) for i in range(owners)]

    def back_of(pairs):
        return [(b, a) for a, b in pairs]

    def move(pieces, perm_of):
        return [pieces[0]] + [lax.ppermute(pieces[k], "tensor", perm_of(k)) for k in range(1, owners)]

    def other_half(x):
        width = x.shape[-1] // 2
        return lax.dynamic_slice_in_dim(x, (1 - side) * width, width, x.ndim - 1)

    tok_pass = other_half(tokens[0])
    listed_other = swap(after(active, tok_pass), "dp").reshape(tiles)
    tok_got = swap(tok_pass, "dp")
    listed = active.reshape(tiles)
    one = jax.ShapeDtypeStruct((1,) + tok_pass.shape[1:], BF16)
    first = functools.partial(first_kernel, owners, tiles)
    tok_first = move(call(first, [one] * owners, 1, moved=2 * tok_pass.size)(listed, tokens[0]), forth)
    meta = plan(listed, listed_other, owners, tiles)
    by_slot = BY_SLOT
    by_position = by_slot + owners * SLOTS
    by_tile = by_position + owners * SLOTS
    cot_pass = other_half(cotangent[0])
    up_keep, up_pass = halves(w_up, side)
    down_keep, down_pass = halves(w_down, side)
    extra_group = (EVEN, EXTRA, False)
    tok_sent = dispatch(meta, tokens[0], tok_got, owners, by_position, ((1, EVEN - 1, True), extra_group))

    def run(center=None):
        fast = center is not None

        def extra_forth(k):
            return [((center - k) % owners, center)]

        def over_subs(part):
            return (part.astype(F32) + swap(part, "sub").astype(F32)).astype(BF16)

        cot_got = swap(cot_pass, "dp")
        if fast:
            tok = [tok_first, move(tok_sent[:owners], forth), move([tok_sent[owners]] * owners, extra_forth)]
            cot_groups = ((0, EVEN, True), extra_group)
            cot_sent = dispatch(meta, cotangent[0], after(cot_got, tok[1][-1]), owners, by_slot, cot_groups)
            cot = [move(cot_sent[:owners], forth), move([cot_sent[owners]] * owners, extra_forth)]
        else:
            cot_groups = ((0, SLOTS, True),)
            tok, cot = [
                [move(dispatch(meta, keep, got, owners, by_slot, cot_groups), forth)]
                for keep, got in ((tokens[0], tok_got), (cotangent[0], cot_got))
            ]
        up = ordered(up_keep, swap(up_pass, "dp"), side, 0)
        down = ordered(down_keep, swap(down_pass, "dp"), side, 0)
        hidden = over_subs(product(meta, tok, up, fast))
        shape = hidden.shape
        positive, squared = call(
            squared_kernel,
            [jax.ShapeDtypeStruct(shape, F32), jax.ShapeDtypeStruct(shape, BF16)],
            2,
            moved=8 * hidden.size,
        )(meta, hidden, swap(hidden, "dp"))
        grad_hidden, home = [None] * len(cot), [None] * len(cot)
        for i in reversed(range(len(cot))):
            first, _, each = cot_groups[i]
            grad_act = over_subs(product(meta, [cot[i]], down, False))
            sums = (grad_act, swap(grad_act, "dp"))
            grad_hidden[i], out = back(meta, positive, sums, up, first, owners)
            perm_of = forth if each else extra_forth
            home[i] = move(out, lambda k: back_of(perm_of(k)))
            down = after(down, grad_hidden[i])
        down_grad, down_other = weights(meta, [squared], cot, False)
        down_got = swap(after(down_other, sums[1]), "dp")
        up_grad, up_other = weights(meta, grad_hidden, tok, fast)
        up_got = swap(up_other, "dp")
        home = [piece for group in home for piece in group]
        mine, other = collect(meta, home, tiles, owners, by_tile)
        return (
            ordered(mine, swap(other, "dp"), side, 2)[None],
            ordered(up_grad, up_got, side, 1),
            ordered(down_grad, down_got, side, 1),
        )

    return lax.switch(
        meta[5],
        [functools.partial(run, center) for center in range(owners)] + [run],
    )


def solution(mesh):
    placed = (
        P(("groups", "dp"), None, "tensor", "sub"),
        P(("groups", "dp"), None, "tensor", "sub"),
        P(("tensor", "dp"), "sub"),
        P(("tensor", "dp"), "sub"),
        P(("groups", "dp"), None, None),
    )
    return jax.shard_map(
        shards,
        mesh=mesh,
        in_specs=placed,
        out_specs=(
            P(("groups", "dp"), None, "tensor", "sub"),
            P(("groups", "tensor", "dp"), "sub"),
            P(("groups", "tensor", "dp"), "sub"),
        ),
        check_vma=False,
    )
```

```python
import functools

import jax
import jax.numpy as jnp
from jax import lax
from jax.experimental import pallas as pl
from jax.experimental.pallas import tpu as pltpu
from jax.sharding import PartitionSpec as P

MOST = 3
EVEN = 2
EXTRA = 2
BY_SLOT = 6
SLOTS = 2 * MOST
F32 = jnp.float32
BF16 = jnp.bfloat16


def swap(x, axis):
    return lax.ppermute(x, axis, [(0, 1), (1, 0)])


def ordered(mine, other, side, axis):
    return jnp.where(
        side == 0,
        jnp.concatenate([mine, other], axis),
        jnp.concatenate([other, mine], axis),
    )


def all_rows(w):
    if lax.axis_size("dp") != 2:
        return lax.all_gather(w, "dp", axis=0, tiled=True)
    return ordered(w, swap(w, "dp"), lax.axis_index("dp"), 0)


def sub_total(part):
    if lax.axis_size("sub") != 2:
        return lax.psum(part.astype(BF16), "sub").astype(F32)
    rounded = part.astype(BF16)
    return rounded.astype(F32) + swap(rounded, "sub").astype(F32)


def replica_total(part):
    if lax.axis_size("dp") != 2:
        return lax.psum_scatter(part.astype(BF16), "dp", scatter_dimension=0, tiled=True)
    side = lax.axis_index("dp")
    n = part.shape[0] // 2
    rounded = part.astype(BF16)
    keep = lax.dynamic_slice_in_dim(rounded, side * n, n, 0)
    pass_on = lax.dynamic_slice_in_dim(rounded, (1 - side) * n, n, 0)
    return (keep.astype(F32) + swap(pass_on, "dp").astype(F32)).astype(BF16)


def plain(tokens, cotangent, w_up, w_down, active):
    tile_count = tokens.shape[1]
    part_rows = tokens.shape[2]
    half_width = tokens.shape[3]
    owners = lax.axis_size("tensor")
    block_ids = active[0]
    owner_list = jnp.arange(owners, dtype=jnp.int32)
    listed = jnp.any(block_ids[:, :, None] == owner_list[None, None, :], axis=1).astype(jnp.int32)
    ranking = jnp.cumsum(listed, axis=0) - 1
    slot_ids = jnp.arange(MOST, dtype=jnp.int32)
    choose = (listed.T[:, None, :] == 1) & (ranking.T[:, None, :] == slot_ids[None, :, None])
    choose_half = choose.astype(BF16)
    choose_full = choose.astype(F32)
    send_tok = jnp.einsum("omt,trd->omrd", choose_half, tokens[0], preferred_element_type=F32).astype(BF16)
    send_cot = jnp.einsum("omt,trd->omrd", choose_half, cotangent[0], preferred_element_type=F32).astype(BF16)
    up_weight_block = all_rows(w_up)
    down_weight_block = all_rows(w_down)
    slot_token = lax.all_to_all(send_tok, "tensor", split_axis=0, concat_axis=2, tiled=True)[0]
    slot_cotangent = lax.all_to_all(send_cot, "tensor", split_axis=0, concat_axis=2, tiled=True)[0]
    hidden = sub_total(jnp.einsum("bkn,vn->bkv", slot_token, up_weight_block, preferred_element_type=F32))
    grad_act = sub_total(jnp.einsum("bkn,vn->bkv", slot_cotangent, down_weight_block, preferred_element_type=F32))
    positive = jnp.maximum(hidden, 0.0)
    squared_activation = (positive * positive).astype(BF16)
    hidden_gradient = (2.0 * positive * grad_act).astype(BF16)
    back_rows = jnp.einsum("opl,la->opa", hidden_gradient, up_weight_block, preferred_element_type=F32).astype(BF16)
    back_rows = back_rows.reshape(MOST, owners, part_rows, half_width)
    received = lax.all_to_all(back_rows, "tensor", split_axis=1, concat_axis=1, tiled=True)
    summed = jnp.einsum("omt,mord->trd", choose_full, received.astype(F32), precision=lax.Precision.HIGHEST)
    grad_tokens = summed.astype(BF16).reshape(1, tile_count, part_rows, half_width)
    up_weight_term = jnp.einsum("epn,epk->nk", hidden_gradient, slot_token, preferred_element_type=F32)
    down_weight_term = jnp.einsum("epn,epk->nk", squared_activation, slot_cotangent, preferred_element_type=F32)
    return grad_tokens, replica_total(up_weight_term), replica_total(down_weight_term)


def after(x, *first):
    return lax.optimization_barrier((x, first))[0]


def halves(x, side):
    width = x.shape[-1] // 2
    keep = lax.dynamic_slice_in_dim(x, side * width, width, x.ndim - 1)
    pass_on = lax.dynamic_slice_in_dim(x, (1 - side) * width, width, x.ndim - 1)
    return keep, pass_on


def copy_rows(src, at, dst, to, start=0):
    step = 512

    @pl.loop(0, dst.shape[-1] // step)
    def _(i):
        cols = pl.ds(pl.multiple_of(i * step, step), step)
        dst[to, :, cols] = src[at, :, pl.ds(pl.multiple_of(start + i * step, step), step)]


def plan_kernel(owners, tiles, mine, other, out):
    side, place = lax.axis_index("dp"), lax.axis_index("tensor")
    block = [jnp.where(side == i // tiles, mine[i % tiles], other[i % tiles]) for i in range(2 * tiles)]
    low = [sum((b == o).astype(jnp.int32) for b in block[:tiles]) for o in range(owners)]
    high = [sum((b == o).astype(jnp.int32) for b in block[tiles:]) for o in range(owners)]
    crowded, most = jnp.int32(0), low[0] + high[0]
    for o in range(1, owners):
        more = low[o] + high[o] > most
        crowded, most = jnp.where(more, o, crowded), jnp.where(more, low[o] + high[o], most)
    fits, mine_count, mine_first, first = most <= EVEN + EXTRA, 0, 0, []
    for o in range(owners):
        count = low[o] + high[o]
        fits = fits & ((o == crowded) | (count <= 1) | ((low[o] == 1) & (high[o] == 1)))
        last = jnp.where(o == crowded, EVEN + EXTRA, EVEN) - 1
        local = jnp.where(side == 0, low[o], high[o])
        first.append(jnp.minimum(jnp.where(local > 0, jnp.where(side == 0, 0, low[o]), last), last))
        mine_count = jnp.where(place == o, count, mine_count)
        mine_first = jnp.where(place == o, first[o], mine_first)
    head = (side, place, crowded, mine_count, mine_first, jnp.where(fits, crowded, owners))
    for i, value in enumerate(head):
        out[i] = value
    by_position, by_tile = BY_SLOT + owners * SLOTS, BY_SLOT + 2 * owners * SLOTS
    for i in range(BY_SLOT, by_tile):
        out[i] = 0
    for i, b in enumerate(block):
        slot = jnp.minimum(sum([(b == c).astype(jnp.int32) for c in block[:i]], jnp.int32(0)), SLOTS - 1)
        start = sum(jnp.where(b == o, first[o], 0) for o in range(owners))
        position = jnp.where(slot == start, 0, jnp.where(slot < start, slot + 1, slot))
        out[BY_SLOT + b * SLOTS + slot] = i
        out[by_position + b * SLOTS + position] = i
        out[by_tile + i] = b
        out[by_tile + 2 * tiles + i] = slot


def plan(mine, other, owners, tiles):
    smem = pl.BlockSpec(memory_space=pltpu.SMEM)
    return pl.pallas_call(
        functools.partial(plan_kernel, owners, tiles),
        out_shape=jax.ShapeDtypeStruct((BY_SLOT + 2 * owners * SLOTS + 4 * tiles,), jnp.int32),
        in_specs=[smem, smem],
        out_specs=smem,
    )(mine, other)


def call(kernel, out_shape, n_vmem, scratch=(), flops=0, moved=0):
    vmem = pl.BlockSpec(memory_space=pltpu.VMEM)
    return pl.pallas_call(
        kernel,
        out_shape=out_shape,
        in_specs=[pl.BlockSpec(memory_space=pltpu.SMEM)] + [vmem] * n_vmem,
        out_specs=[vmem] * len(out_shape),
        scratch_shapes=list(scratch),
        compiler_params=pltpu.CompilerParams(vmem_limit_bytes=40 << 20),
        cost_estimate=pl.CostEstimate(flops=flops, bytes_accessed=moved, transcendentals=0),
    )


def dispatch_kernel(owners, tiles, base, groups, meta, keep, got, *outs):
    side, place, crowded = meta[0], meta[1], meta[2]
    n = 0
    for first, count, each in groups:
        for k in range(owners if each else 1):
            owner = lax.rem(place + k, owners) if each else crowded
            out = outs[n]

            @pl.loop(0, count)
            def _(s):
                tile = meta[base + owner * SLOTS + first + s]
                own = lax.div(tile, tiles) == side
                at = lax.rem(tile, tiles)

                @pl.when(own)
                def _():
                    copy_rows(keep, at, out, s, side * out.shape[2])

                @pl.when(jnp.logical_not(own))
                def _():
                    copy_rows(got, at, out, s)

            n += 1


def dispatch(meta, keep, got, owners, base, groups):
    tiles, rows, width = got.shape
    counts = [count for _, count, each in groups for _ in range(owners if each else 1)]
    outs = [jax.ShapeDtypeStruct((c, rows, width), got.dtype) for c in counts]
    kernel = functools.partial(dispatch_kernel, owners, tiles, base, groups)
    return call(kernel, outs, 2, moved=4 * sum(counts) * rows * width)(meta, keep, got)


def first_kernel(owners, tiles, listed, keep, *outs):
    side, place = lax.axis_index("dp"), lax.axis_index("tensor")
    for k in range(owners):
        owner = lax.rem(place + k, owners)
        at = jnp.int32(0)
        for t in reversed(range(tiles)):
            at = jnp.where(listed[t] == owner, t, at)
        copy_rows(keep, at, outs[k], 0, side * outs[k].shape[2])


def rows_of(pieces, counts, owners, cols):
    parts, n = [], 0
    for count in counts:
        for s in range(count):
            parts += [pieces[n + k][s, :, cols] for k in range(owners)]
        n += owners
    return jnp.concatenate(parts, 0)


def product_kernel(counts, owners, moved, meta, *rest):
    pieces, weight, out, total = rest[:-3], rest[-3], rest[-2], rest[-1]
    step = 512
    total[...] = jnp.zeros_like(total)

    @pl.loop(0, weight.shape[1] // step)
    def _(i):
        cols = pl.ds(pl.multiple_of(i * step, step), step)
        total[...] += lax.dot_general(
            rows_of(pieces, counts, owners, cols),
            weight[:, cols],
            (((1,), (1,)), ((), ())),
            preferred_element_type=F32,
        )

    n = out.shape[1]
    for p in range(sum(counts)):
        out[slot_at(meta[4], p) if moved else p] = total[p * n : (p + 1) * n].astype(BF16)


def slot_at(first, p):
    return first if p == 0 else jnp.where(p <= first, p - 1, p)


def product(meta, groups, weight, moved):
    owners = len(groups[0])
    counts = [g[0].shape[0] for g in groups]
    pieces = [p for g in groups for p in g]
    n, m, rows = sum(counts), weight.shape[0], pieces[0].shape[1] * owners
    return call(
        functools.partial(product_kernel, counts, owners, moved),
        [jax.ShapeDtypeStruct((n, rows, m), BF16)],
        len(pieces) + 1,
        [pltpu.VMEM((n * rows, m), F32)],
        flops=2 * n * rows * m * weight.shape[1],
        moved=2 * (n * rows + m) * weight.shape[1],
    )(meta, *pieces, weight)[0]


def squared_kernel(meta, h1, h2, positive, squared):
    for s in range(h1.shape[0]):
        h = jnp.maximum(h1[s].astype(F32) + h2[s].astype(F32), 0.0)
        h = jnp.where(s < meta[3], h, 0.0)
        positive[s] = h
        squared[s] = (h * h).astype(BF16)


def back_kernel(first, count, owners, parts, meta, positive, *rest):
    g, up, grad_hidden, outs = rest[:parts], rest[parts], rest[parts + 1], rest[parts + 2 :]
    n, m = g[0].shape[1], g[0].shape[2]
    rows = n // owners
    for s in range(count):
        grad_act = sum(part[s].astype(F32) for part in g)
        grad_hidden[s] = (2.0 * positive[first + s] * grad_act).astype(BF16)
    step = 512

    @pl.loop(0, up.shape[1] // step)
    def _(i):
        cols = pl.ds(pl.multiple_of(i * step, step), step)
        out = jnp.dot(
            grad_hidden[...].reshape(count * n, m), up[:, cols], preferred_element_type=F32
        ).astype(BF16)
        for s in range(count):
            for k in range(owners):
                at = s * n + k * rows
                outs[k][s, :, cols] = out[at : at + rows]


def back(meta, positive, g, up, first, owners):
    count, n, m = g[0].shape
    width = up.shape[1]
    outs = call(
        functools.partial(back_kernel, first, count, owners, len(g)),
        [jax.ShapeDtypeStruct((count, n, m), BF16)]
        + [jax.ShapeDtypeStruct((count, n // owners, width), BF16)] * owners,
        2 + len(g),
        flops=2 * count * n * m * width,
        moved=2 * (count * n + m) * width,
    )(meta, positive, *g, up)
    return outs[0], list(outs[1:])


def weights_kernel(owners, act_counts, counts, moved, meta, *rest):
    acts, data, rest = rest[: len(act_counts)], rest[len(act_counts) : -4], rest[-4:]
    keep, pass_on, by_slot, turned = rest
    side = meta[0]
    n, m = acts[0].shape[1], acts[0].shape[2]
    p = 0
    for act, count in zip(acts, act_counts):
        by_slot[p : p + count] = act[...]
        p += count
    for p in range(sum(counts)):
        turned[:, p * n : (p + 1) * n] = by_slot[slot_at(meta[4], p) if moved else p].T
    step = 256

    @pl.loop(0, keep.shape[1] // step)
    def _(i):
        cols = pl.ds(pl.multiple_of(i * step, step), step)
        g = jnp.dot(turned[...], rows_of(data, counts, owners, cols), preferred_element_type=F32)
        low, high = g[: m // 2].astype(BF16), g[m // 2 :].astype(BF16)
        keep[:, cols] = jnp.where(side == 0, low, high)
        pass_on[:, cols] = jnp.where(side == 0, high, low)


def weights(meta, acts, groups, moved):
    owners = len(groups[0])
    act_counts, counts = [a.shape[0] for a in acts], [g[0].shape[0] for g in groups]
    data = [p for g in groups for p in g]
    _, n, m = acts[0].shape
    slots, width = sum(counts), data[0].shape[2]
    return call(
        functools.partial(weights_kernel, owners, act_counts, counts, moved),
        [jax.ShapeDtypeStruct((m // 2, width), BF16)] * 2,
        len(acts) + len(data),
        [pltpu.VMEM((slots, n, m), BF16), pltpu.VMEM((m, slots * n), BF16)],
        flops=2 * slots * n * m * width,
        moved=2 * (slots * n + m) * width,
    )(meta, *acts, *data)


def collect_kernel(owners, tiles, base, meta, *rest):
    pieces, (mine, other) = rest[:-2], rest[-2:]
    side, place = meta[0], meta[1]
    even = pieces[0].shape[0]
    for r, out in enumerate((mine, other)):
        replica = side if r == 0 else 1 - side

        @pl.loop(0, tiles)
        def _(t):
            tile = replica * tiles + t
            k = lax.rem(meta[base + tile] - place + owners, owners)
            slot = meta[base + 2 * tiles + tile]
            for kk in range(owners):

                @pl.when((k == kk) & (slot < even))
                def _():
                    copy_rows(pieces[kk], slot, out, t)

                if len(pieces) > owners:

                    @pl.when((k == kk) & (slot >= even))
                    def _():
                        copy_rows(pieces[owners + kk], slot - even, out, t)


def collect(meta, pieces, tiles, owners, base):
    _, rows, width = pieces[0].shape
    kernel = functools.partial(collect_kernel, owners, tiles, base)
    outs = [jax.ShapeDtypeStruct((tiles, rows, width), BF16)] * 2
    return call(kernel, outs, len(pieces), moved=8 * tiles * rows * width)(meta, *pieces)


def shards(tokens, cotangent, w_up, w_down, active):
    owners = lax.axis_size("tensor")
    replicas = lax.axis_size("dp")
    subs = lax.axis_size("sub")
    if replicas != 2 or subs != 2 or active.shape[2] != 1 or tokens.shape[2] % 16:
        return plain(tokens, cotangent, w_up, w_down, active)
    tiles = tokens.shape[1]
    rows = tokens.shape[2]
    side = lax.axis_index("dp")
    place = lax.axis_index("tensor")
    def forth(k):
        return [(i, (i + k) % owners) for i in range(owners)]

    def back_of(pairs):
        return [(b, a) for a, b in pairs]

    def move(pieces, perm_of):
        return [pieces[0]] + [lax.ppermute(pieces[k], "tensor", perm_of(k)) for k in range(1, owners)]

    def other_half(x):
        width = x.shape[-1] // 2
        return lax.dynamic_slice_in_dim(x, (1 - side) * width, width, x.ndim - 1)

    tok_pass = other_half(tokens[0])
    listed_other = swap(after(active, tok_pass), "dp").reshape(tiles)
    tok_got = swap(tok_pass, "dp")
    listed = active.reshape(tiles)
    one = jax.ShapeDtypeStruct((1,) + tok_pass.shape[1:], BF16)
    first = functools.partial(first_kernel, owners, tiles)
    tok_first = move(call(first, [one] * owners, 1, moved=2 * tok_pass.size)(listed, tokens[0]), forth)
    meta = plan(listed, listed_other, owners, tiles)
    by_slot = BY_SLOT
    by_position = by_slot + owners * SLOTS
    by_tile = by_position + owners * SLOTS
    cot_pass = other_half(cotangent[0])
    up_keep, up_pass = halves(w_up, side)
    down_keep, down_pass = halves(w_down, side)
    extra_group = (EVEN, EXTRA, False)
    tok_sent = dispatch(meta, tokens[0], tok_got, owners, by_position, ((1, EVEN - 1, True), extra_group))

    def run(center=None):
        fast = center is not None

        def extra_forth(k):
            return [((center - k) % owners, center)]

        def over_subs(part):
            return (part.astype(F32) + swap(part, "sub").astype(F32)).astype(BF16)

        cot_got = swap(cot_pass, "dp")
        if fast:
            tok = [tok_first, move(tok_sent[:owners], forth), move([tok_sent[owners]] * owners, extra_forth)]
            cot_groups = ((0, EVEN, True), extra_group)
            cot_sent = dispatch(meta, cotangent[0], after(cot_got, tok[1][-1]), owners, by_slot, cot_groups)
            cot = [move(cot_sent[:owners], forth), move([cot_sent[owners]] * owners, extra_forth)]
        else:
            cot_groups = ((0, SLOTS, True),)
            tok, cot = [
                [move(dispatch(meta, keep, got, owners, by_slot, cot_groups), forth)]
                for keep, got in ((tokens[0], tok_got), (cotangent[0], cot_got))
            ]
        up = ordered(up_keep, swap(up_pass, "dp"), side, 0)
        down = ordered(down_keep, swap(down_pass, "dp"), side, 0)
        hidden = over_subs(product(meta, tok, up, fast))
        shape = hidden.shape
        positive, squared = call(
            squared_kernel,
            [jax.ShapeDtypeStruct(shape, F32), jax.ShapeDtypeStruct(shape, BF16)],
            2,
            moved=8 * hidden.size,
        )(meta, hidden, swap(hidden, "dp"))
        grad_hidden, home, sent_back = [None] * len(cot), [None] * len(cot), ()
        for i in reversed(range(len(cot))):
            first, _, each = cot_groups[i]
            grad_act = product(meta, [cot[i]], down, False)
            if i == 0:
                crossed = lax.ppermute(grad_act, ("dp", "sub"), [(0, 3), (3, 0), (1, 2), (2, 1)])
                sums = (grad_act, swap(grad_act, "dp"), crossed, swap(grad_act, "sub"))
            else:
                grad_act = over_subs(grad_act)
                sums = (grad_act, swap(grad_act, "dp"))
            grad_hidden[i], out = back(meta, after(positive, sent_back), sums, up, first, owners)
            perm_of = forth if each else extra_forth
            home[i] = move(out, lambda k: back_of(perm_of(k)))
            sent_back = home[i][1]
            down = after(down, grad_hidden[i])
        down_grad, down_other = weights(meta, [after(squared, *grad_hidden)], cot, False)
        down_got = swap(down_other, "dp")
        up_grad, up_other = weights(meta, grad_hidden, tok, fast)
        up_got = swap(up_other, "dp")
        home = [piece for group in home for piece in group]
        mine, other = collect(meta, home, tiles, owners, by_tile)
        return (
            ordered(mine, swap(other, "dp"), side, 2)[None],
            ordered(up_grad, up_got, side, 1),
            ordered(down_grad, down_got, side, 1),
        )

    return lax.switch(
        meta[5],
        [functools.partial(run, center) for center in range(owners)] + [run],
    )


def solution(mesh):
    placed = (
        P(("groups", "dp"), None, "tensor", "sub"),
        P(("groups", "dp"), None, "tensor", "sub"),
        P(("tensor", "dp"), "sub"),
        P(("tensor", "dp"), "sub"),
        P(("groups", "dp"), None, None),
    )
    return jax.shard_map(
        shards,
        mesh=mesh,
        in_specs=placed,
        out_specs=(
            P(("groups", "dp"), None, "tensor", "sub"),
            P(("groups", "tensor", "dp"), "sub"),
            P(("groups", "tensor", "dp"), "sub"),
        ),
        check_vma=False,
    )
```

```python
import functools

import jax
import jax.numpy as jnp
from jax import lax
from jax.experimental import pallas as pl
from jax.experimental.pallas import tpu as pltpu
from jax.sharding import PartitionSpec as P

MOST = 3
EVEN = 2
EXTRA = 2
BY_SLOT = 6
SLOTS = 2 * MOST
F32 = jnp.float32
BF16 = jnp.bfloat16


def swap(x, axis):
    return lax.ppermute(x, axis, [(0, 1), (1, 0)])


def ordered(mine, other, side, axis):
    return jnp.where(
        side == 0,
        jnp.concatenate([mine, other], axis),
        jnp.concatenate([other, mine], axis),
    )


def all_rows(w):
    if lax.axis_size("dp") != 2:
        return lax.all_gather(w, "dp", axis=0, tiled=True)
    return ordered(w, swap(w, "dp"), lax.axis_index("dp"), 0)


def sub_total(part):
    if lax.axis_size("sub") != 2:
        return lax.psum(part.astype(BF16), "sub").astype(F32)
    rounded = part.astype(BF16)
    return rounded.astype(F32) + swap(rounded, "sub").astype(F32)


def replica_total(part):
    if lax.axis_size("dp") != 2:
        return lax.psum_scatter(part.astype(BF16), "dp", scatter_dimension=0, tiled=True)
    side = lax.axis_index("dp")
    n = part.shape[0] // 2
    rounded = part.astype(BF16)
    keep = lax.dynamic_slice_in_dim(rounded, side * n, n, 0)
    pass_on = lax.dynamic_slice_in_dim(rounded, (1 - side) * n, n, 0)
    return (keep.astype(F32) + swap(pass_on, "dp").astype(F32)).astype(BF16)


def plain(tokens, cotangent, w_up, w_down, active):
    tile_count = tokens.shape[1]
    part_rows = tokens.shape[2]
    half_width = tokens.shape[3]
    owners = lax.axis_size("tensor")
    block_ids = active[0]
    owner_list = jnp.arange(owners, dtype=jnp.int32)
    listed = jnp.any(block_ids[:, :, None] == owner_list[None, None, :], axis=1).astype(jnp.int32)
    ranking = jnp.cumsum(listed, axis=0) - 1
    slot_ids = jnp.arange(MOST, dtype=jnp.int32)
    choose = (listed.T[:, None, :] == 1) & (ranking.T[:, None, :] == slot_ids[None, :, None])
    choose_half = choose.astype(BF16)
    choose_full = choose.astype(F32)
    send_tok = jnp.einsum("omt,trd->omrd", choose_half, tokens[0], preferred_element_type=F32).astype(BF16)
    send_cot = jnp.einsum("omt,trd->omrd", choose_half, cotangent[0], preferred_element_type=F32).astype(BF16)
    up_weight_block = all_rows(w_up)
    down_weight_block = all_rows(w_down)
    slot_token = lax.all_to_all(send_tok, "tensor", split_axis=0, concat_axis=2, tiled=True)[0]
    slot_cotangent = lax.all_to_all(send_cot, "tensor", split_axis=0, concat_axis=2, tiled=True)[0]
    hidden = sub_total(jnp.einsum("bkn,vn->bkv", slot_token, up_weight_block, preferred_element_type=F32))
    grad_act = sub_total(jnp.einsum("bkn,vn->bkv", slot_cotangent, down_weight_block, preferred_element_type=F32))
    positive = jnp.maximum(hidden, 0.0)
    squared_activation = (positive * positive).astype(BF16)
    hidden_gradient = (2.0 * positive * grad_act).astype(BF16)
    back_rows = jnp.einsum("opl,la->opa", hidden_gradient, up_weight_block, preferred_element_type=F32).astype(BF16)
    back_rows = back_rows.reshape(MOST, owners, part_rows, half_width)
    received = lax.all_to_all(back_rows, "tensor", split_axis=1, concat_axis=1, tiled=True)
    summed = jnp.einsum("omt,mord->trd", choose_full, received.astype(F32), precision=lax.Precision.HIGHEST)
    grad_tokens = summed.astype(BF16).reshape(1, tile_count, part_rows, half_width)
    up_weight_term = jnp.einsum("epn,epk->nk", hidden_gradient, slot_token, preferred_element_type=F32)
    down_weight_term = jnp.einsum("epn,epk->nk", squared_activation, slot_cotangent, preferred_element_type=F32)
    return grad_tokens, replica_total(up_weight_term), replica_total(down_weight_term)


def after(x, *first):
    return lax.optimization_barrier((x, first))[0]


def halves(x, side):
    width = x.shape[-1] // 2
    keep = lax.dynamic_slice_in_dim(x, side * width, width, x.ndim - 1)
    pass_on = lax.dynamic_slice_in_dim(x, (1 - side) * width, width, x.ndim - 1)
    return keep, pass_on


def copy_rows(src, at, dst, to, start=0):
    step = 512

    @pl.loop(0, dst.shape[-1] // step)
    def _(i):
        cols = pl.ds(pl.multiple_of(i * step, step), step)
        dst[to, :, cols] = src[at, :, pl.ds(pl.multiple_of(start + i * step, step), step)]


def plan_kernel(owners, tiles, mine, other, out):
    side, place = lax.axis_index("dp"), lax.axis_index("tensor")
    block = [jnp.where(side == i // tiles, mine[i % tiles], other[i % tiles]) for i in range(2 * tiles)]
    low = [sum((b == o).astype(jnp.int32) for b in block[:tiles]) for o in range(owners)]
    high = [sum((b == o).astype(jnp.int32) for b in block[tiles:]) for o in range(owners)]
    crowded, most = jnp.int32(0), low[0] + high[0]
    for o in range(1, owners):
        more = low[o] + high[o] > most
        crowded, most = jnp.where(more, o, crowded), jnp.where(more, low[o] + high[o], most)
    fits, mine_count, mine_first, first = most <= EVEN + EXTRA, 0, 0, []
    for o in range(owners):
        count = low[o] + high[o]
        fits = fits & ((o == crowded) | (count <= 1) | ((low[o] == 1) & (high[o] == 1)))
        last = jnp.where(o == crowded, EVEN + EXTRA, EVEN) - 1
        local = jnp.where(side == 0, low[o], high[o])
        first.append(jnp.minimum(jnp.where(local > 0, jnp.where(side == 0, 0, low[o]), last), last))
        mine_count = jnp.where(place == o, count, mine_count)
        mine_first = jnp.where(place == o, first[o], mine_first)
    head = (side, place, crowded, mine_count, mine_first, jnp.where(fits, crowded, owners))
    for i, value in enumerate(head):
        out[i] = value
    by_position, by_tile = BY_SLOT + owners * SLOTS, BY_SLOT + 2 * owners * SLOTS
    for i in range(BY_SLOT, by_tile):
        out[i] = 0
    for i, b in enumerate(block):
        slot = jnp.minimum(sum([(b == c).astype(jnp.int32) for c in block[:i]], jnp.int32(0)), SLOTS - 1)
        start = sum(jnp.where(b == o, first[o], 0) for o in range(owners))
        position = jnp.where(slot == start, 0, jnp.where(slot < start, slot + 1, slot))
        out[BY_SLOT + b * SLOTS + slot] = i
        out[by_position + b * SLOTS + position] = i
        out[by_tile + i] = b
        out[by_tile + 2 * tiles + i] = slot


def plan(mine, other, owners, tiles):
    smem = pl.BlockSpec(memory_space=pltpu.SMEM)
    return pl.pallas_call(
        functools.partial(plan_kernel, owners, tiles),
        out_shape=jax.ShapeDtypeStruct((BY_SLOT + 2 * owners * SLOTS + 4 * tiles,), jnp.int32),
        in_specs=[smem, smem],
        out_specs=smem,
    )(mine, other)


def call(kernel, out_shape, n_vmem, scratch=(), flops=0, moved=0):
    vmem = pl.BlockSpec(memory_space=pltpu.VMEM)
    return pl.pallas_call(
        kernel,
        out_shape=out_shape,
        in_specs=[pl.BlockSpec(memory_space=pltpu.SMEM)] + [vmem] * n_vmem,
        out_specs=[vmem] * len(out_shape),
        scratch_shapes=list(scratch),
        compiler_params=pltpu.CompilerParams(vmem_limit_bytes=40 << 20),
        cost_estimate=pl.CostEstimate(flops=flops, bytes_accessed=moved, transcendentals=0),
    )


def dispatch_kernel(owners, tiles, base, groups, meta, keep, got, *outs):
    side, place, crowded = meta[0], meta[1], meta[2]
    n = 0
    for first, count, each in groups:
        for k in range(owners if each else 1):
            owner = lax.rem(place + k, owners) if each else crowded
            out = outs[n]

            @pl.loop(0, count)
            def _(s):
                tile = meta[base + owner * SLOTS + first + s]
                own = lax.div(tile, tiles) == side
                at = lax.rem(tile, tiles)

                @pl.when(own)
                def _():
                    copy_rows(keep, at, out, s, side * out.shape[2])

                @pl.when(jnp.logical_not(own))
                def _():
                    copy_rows(got, at, out, s)

            n += 1


def dispatch(meta, keep, got, owners, base, groups):
    tiles, rows, width = got.shape
    counts = [count for _, count, each in groups for _ in range(owners if each else 1)]
    outs = [jax.ShapeDtypeStruct((c, rows, width), got.dtype) for c in counts]
    kernel = functools.partial(dispatch_kernel, owners, tiles, base, groups)
    return call(kernel, outs, 2, moved=4 * sum(counts) * rows * width)(meta, keep, got)


def first_kernel(owners, tiles, listed, keep, *outs):
    side, place = lax.axis_index("dp"), lax.axis_index("tensor")
    for k in range(owners):
        owner = lax.rem(place + k, owners)
        at = jnp.int32(0)
        for t in reversed(range(tiles)):
            at = jnp.where(listed[t] == owner, t, at)
        copy_rows(keep, at, outs[k], 0, side * outs[k].shape[2])


def rows_of(pieces, counts, owners, cols):
    parts, n = [], 0
    for count in counts:
        for s in range(count):
            parts += [pieces[n + k][s, :, cols] for k in range(owners)]
        n += owners
    return jnp.concatenate(parts, 0)


def product_kernel(counts, owners, moved, meta, *rest):
    pieces, weight, out, total = rest[:-3], rest[-3], rest[-2], rest[-1]
    step = 512
    total[...] = jnp.zeros_like(total)

    @pl.loop(0, weight.shape[1] // step)
    def _(i):
        cols = pl.ds(pl.multiple_of(i * step, step), step)
        total[...] += lax.dot_general(
            rows_of(pieces, counts, owners, cols),
            weight[:, cols],
            (((1,), (1,)), ((), ())),
            preferred_element_type=F32,
        )

    n = out.shape[1]
    for p in range(sum(counts)):
        out[slot_at(meta[4], p) if moved else p] = total[p * n : (p + 1) * n].astype(BF16)


def slot_at(first, p):
    return first if p == 0 else jnp.where(p <= first, p - 1, p)


def product(meta, groups, weight, moved):
    owners = len(groups[0])
    counts = [g[0].shape[0] for g in groups]
    pieces = [p for g in groups for p in g]
    n, m, rows = sum(counts), weight.shape[0], pieces[0].shape[1] * owners
    return call(
        functools.partial(product_kernel, counts, owners, moved),
        [jax.ShapeDtypeStruct((n, rows, m), BF16)],
        len(pieces) + 1,
        [pltpu.VMEM((n * rows, m), F32)],
        flops=2 * n * rows * m * weight.shape[1],
        moved=2 * (n * rows + m) * weight.shape[1],
    )(meta, *pieces, weight)[0]


def squared_kernel(meta, h1, h2, positive, squared):
    for s in range(h1.shape[0]):
        h = jnp.maximum(h1[s].astype(F32) + h2[s].astype(F32), 0.0)
        h = jnp.where(s < meta[3], h, 0.0)
        positive[s] = h
        squared[s] = (h * h).astype(BF16)


def back_kernel(first, count, owners, meta, positive, g1, g2, up, grad_hidden, *outs):
    n, m = g1.shape[1], g1.shape[2]
    rows = n // owners
    for s in range(count):
        grad_act = g1[s].astype(F32) + g2[s].astype(F32)
        grad_hidden[s] = (2.0 * positive[first + s] * grad_act).astype(BF16)
    step = 512

    @pl.loop(0, up.shape[1] // step)
    def _(i):
        cols = pl.ds(pl.multiple_of(i * step, step), step)
        out = jnp.dot(
            grad_hidden[...].reshape(count * n, m), up[:, cols], preferred_element_type=F32
        ).astype(BF16)
        for s in range(count):
            for k in range(owners):
                at = s * n + k * rows
                outs[k][s, :, cols] = out[at : at + rows]


def back(meta, positive, g, up, first, owners):
    count, n, m = g[0].shape
    width = up.shape[1]
    outs = call(
        functools.partial(back_kernel, first, count, owners),
        [jax.ShapeDtypeStruct((count, n, m), BF16)]
        + [jax.ShapeDtypeStruct((count, n // owners, width), BF16)] * owners,
        4,
        flops=2 * count * n * m * width,
        moved=2 * (count * n + m) * width,
    )(meta, positive, *g, up)
    return outs[0], list(outs[1:])


def weights_kernel(owners, act_counts, counts, moved, meta, *rest):
    acts, data, rest = rest[: len(act_counts)], rest[len(act_counts) : -4], rest[-4:]
    keep, pass_on, by_slot, turned = rest
    side = meta[0]
    n, m = acts[0].shape[1], acts[0].shape[2]
    p = 0
    for act, count in zip(acts, act_counts):
        by_slot[p : p + count] = act[...]
        p += count
    for p in range(sum(counts)):
        turned[:, p * n : (p + 1) * n] = by_slot[slot_at(meta[4], p) if moved else p].T
    step = 256

    @pl.loop(0, keep.shape[1] // step)
    def _(i):
        cols = pl.ds(pl.multiple_of(i * step, step), step)
        g = jnp.dot(turned[...], rows_of(data, counts, owners, cols), preferred_element_type=F32)
        low, high = g[: m // 2].astype(BF16), g[m // 2 :].astype(BF16)
        keep[:, cols] = jnp.where(side == 0, low, high)
        pass_on[:, cols] = jnp.where(side == 0, high, low)


def weights(meta, acts, groups, moved):
    owners = len(groups[0])
    act_counts, counts = [a.shape[0] for a in acts], [g[0].shape[0] for g in groups]
    data = [p for g in groups for p in g]
    _, n, m = acts[0].shape
    slots, width = sum(counts), data[0].shape[2]
    return call(
        functools.partial(weights_kernel, owners, act_counts, counts, moved),
        [jax.ShapeDtypeStruct((m // 2, width), BF16)] * 2,
        len(acts) + len(data),
        [pltpu.VMEM((slots, n, m), BF16), pltpu.VMEM((m, slots * n), BF16)],
        flops=2 * slots * n * m * width,
        moved=2 * (slots * n + m) * width,
    )(meta, *acts, *data)


def collect_kernel(owners, tiles, base, own, meta, *rest):
    pieces, out = rest[:-1], rest[-1]
    side, place = meta[0], meta[1]
    even = pieces[0].shape[0]
    replica = side if own else 1 - side

    @pl.loop(0, tiles)
    def _(t):
        tile = replica * tiles + t
        k = lax.rem(meta[base + tile] - place + owners, owners)
        slot = meta[base + 2 * tiles + tile]
        for kk in range(owners):

            @pl.when((k == kk) & (slot < even))
            def _():
                copy_rows(pieces[kk], slot, out, t)

            if len(pieces) > owners:

                @pl.when((k == kk) & (slot >= even))
                def _():
                    copy_rows(pieces[owners + kk], slot - even, out, t)


def collect(meta, pieces, tiles, owners, base, own):
    _, rows, width = pieces[0].shape
    kernel = functools.partial(collect_kernel, owners, tiles, base, own)
    outs = [jax.ShapeDtypeStruct((tiles, rows, width), BF16)]
    return call(kernel, outs, len(pieces), moved=4 * tiles * rows * width)(meta, *pieces)[0]


def shards(tokens, cotangent, w_up, w_down, active):
    owners = lax.axis_size("tensor")
    replicas = lax.axis_size("dp")
    subs = lax.axis_size("sub")
    if replicas != 2 or subs != 2 or active.shape[2] != 1 or tokens.shape[2] % 16:
        return plain(tokens, cotangent, w_up, w_down, active)
    tiles = tokens.shape[1]
    rows = tokens.shape[2]
    side = lax.axis_index("dp")
    place = lax.axis_index("tensor")
    def forth(k):
        return [(i, (i + k) % owners) for i in range(owners)]

    def back_of(pairs):
        return [(b, a) for a, b in pairs]

    def move(pieces, perm_of):
        return [pieces[0]] + [lax.ppermute(pieces[k], "tensor", perm_of(k)) for k in range(1, owners)]

    def other_half(x):
        width = x.shape[-1] // 2
        return lax.dynamic_slice_in_dim(x, (1 - side) * width, width, x.ndim - 1)

    tok_pass = other_half(tokens[0])
    listed_other = swap(after(active, tok_pass), "dp").reshape(tiles)
    tok_got = swap(tok_pass, "dp")
    listed = active.reshape(tiles)
    one = jax.ShapeDtypeStruct((1,) + tok_pass.shape[1:], BF16)
    first = functools.partial(first_kernel, owners, tiles)
    tok_first = move(call(first, [one] * owners, 1, moved=2 * tok_pass.size)(listed, tokens[0]), forth)
    meta = plan(listed, listed_other, owners, tiles)
    by_slot = BY_SLOT
    by_position = by_slot + owners * SLOTS
    by_tile = by_position + owners * SLOTS
    cot_pass = other_half(cotangent[0])
    up_keep, up_pass = halves(w_up, side)
    down_keep, down_pass = halves(w_down, side)
    extra_group = (EVEN, EXTRA, False)
    tok_sent = dispatch(meta, tokens[0], tok_got, owners, by_position, ((1, EVEN - 1, True), extra_group))

    def run(center=None):
        fast = center is not None

        def extra_forth(k):
            return [((center - k) % owners, center)]

        def over_subs(part):
            return (part.astype(F32) + swap(part, "sub").astype(F32)).astype(BF16)

        cot_got = swap(cot_pass, "dp")
        if fast:
            tok = [tok_first, move(tok_sent[:owners], forth), move([tok_sent[owners]] * owners, extra_forth)]
            cot_groups = ((0, EVEN, True), extra_group)
            cot_sent = dispatch(meta, cotangent[0], after(cot_got, tok[1][-1]), owners, by_slot, cot_groups)
            cot = [move(cot_sent[:owners], forth), move([cot_sent[owners]] * owners, extra_forth)]
        else:
            cot_groups = ((0, SLOTS, True),)
            tok, cot = [
                [move(dispatch(meta, keep, got, owners, by_slot, cot_groups), forth)]
                for keep, got in ((tokens[0], tok_got), (cotangent[0], cot_got))
            ]
        up = ordered(up_keep, swap(up_pass, "dp"), side, 0)
        down = ordered(down_keep, swap(down_pass, "dp"), side, 0)
        hidden = over_subs(product(meta, tok, up, fast))
        shape = hidden.shape
        positive, squared = call(
            squared_kernel,
            [jax.ShapeDtypeStruct(shape, F32), jax.ShapeDtypeStruct(shape, BF16)],
            2,
            moved=8 * hidden.size,
        )(meta, hidden, swap(hidden, "dp"))
        grad_hidden, home = [None] * len(cot), [None] * len(cot)
        for i in reversed(range(len(cot))):
            first, _, each = cot_groups[i]
            grad_act = over_subs(product(meta, [cot[i]], down, False))
            sums = (grad_act, swap(grad_act, "dp"))
            grad_hidden[i], out = back(meta, positive, sums, up, first, owners)
            perm_of = forth if each else extra_forth
            home[i] = move(out, lambda k: back_of(perm_of(k)))
            down = after(down, grad_hidden[i])
        down_grad, down_other = weights(meta, [squared], cot, False)
        down_got = swap(after(down_other, sums[1]), "dp")
        up_grad, up_other = weights(meta, grad_hidden, tok, fast)
        up_got = swap(up_other, "dp")
        home = [piece for group in home for piece in group]
        other = collect(meta, home, tiles, owners, by_tile, False)
        mine = collect(after(meta, other), home, tiles, owners, by_tile, True)
        return (
            ordered(mine, swap(other, "dp"), side, 2)[None],
            ordered(up_grad, up_got, side, 1),
            ordered(down_grad, down_got, side, 1),
        )

    return lax.switch(
        meta[5],
        [functools.partial(run, center) for center in range(owners)] + [run],
    )


def solution(mesh):
    placed = (
        P(("groups", "dp"), None, "tensor", "sub"),
        P(("groups", "dp"), None, "tensor", "sub"),
        P(("tensor", "dp"), "sub"),
        P(("tensor", "dp"), "sub"),
        P(("groups", "dp"), None, None),
    )
    return jax.shard_map(
        shards,
        mesh=mesh,
        in_specs=placed,
        out_specs=(
            P(("groups", "dp"), None, "tensor", "sub"),
            P(("groups", "tensor", "dp"), "sub"),
            P(("groups", "tensor", "dp"), "sub"),
        ),
        check_vma=False,
    )
```
